32 devices in a mesh: region: 8 (over z, x), eig: 4 (over y, core).
Axes of the slice: x: 2, y: 2, z: 4, core: 2. Of those that a mesh axis runs over, the one named last changes fastest.
Arguments:
- residual: float32 [2, 192, 32, 3072], P(None, 'region', None, 'eig'), may hold values from -6 to 6
- basis: float32 [2, 192, 64, 3072], P(None, 'region', None, 'eig'), may hold values from -0.078125 to 0.078125
- eigvecs: bfloat16 [2, 192, 64, 1024], P(None, 'region', None, 'eig'), may hold values from -0.0390625 to 0.0390625
- weights: float32 [1024], P('eig'), may hold values from 6 to 24
Outputs:
- correction: float32 [2, 192, 32, 3072], P(None, 'region', None, 'eig')
The draws below stay inside these ranges and needn't reach their ends.
All inputs are finite; a program needn't handle non-finite values.
Results may differ from the reference program's by a relative error of at most 0.013.
Values may be sent and summed in bfloat16 or wider, within the bound.
No kernel may reach another device: no remote copies, remote signals or barrier semaphores. Data moves between devices by JAX's collectives and lax.ppermute only.
A program may use at most 64 MiB of HBM per device.

```python
import math
import jax
import jax.numpy as jnp
from jax import lax

COMP = 3072
BASIS = 64
EIGVEC = 1024
COLS = 32
BLOCKS = 192


def level_of(rng, extent, split, smallest, largest):
    factor_of = 1.0
    for dim, shards_of in split:
        steps = jax.random.uniform(jax.random.fold_in(jax.random.fold_in(rng, 6), dim), (shards_of,), jnp.float32, smallest / len(split), largest / len(split))
        factor_of = factor_of * jnp.repeat(jnp.exp(steps), extent[dim] // shards_of).reshape((-1,) + (1,) * (len(extent) - 1 - dim))
    return factor_of


def bell_draw(key, shape, scale, limit, shards=(), held_as=jnp.bfloat16):
    array = scale * jax.random.normal(key, shape, jnp.float32)
    if shards:
        array = array * level_of(key, shape, shards, -0.22, 0.18)
    return jnp.clip(array, -limit, limit).astype(held_as)


def setup_inputs(seed: int = 0) -> dict:
    splits = jax.random.split(jax.random.key(seed), 5)
    return {
        "residual": bell_draw(splits[0], (2, BLOCKS, COLS, COMP), 1.0, 6.0, ((1, 8), (3, 4)), jnp.float32),
        "basis": bell_draw(splits[1], (2, BLOCKS, BASIS, COMP), (2 * COMP) ** -0.5, 0.078125, ((1, 8), (3, 4)), jnp.float32),
        "eigvecs": bell_draw(splits[2], (2, BLOCKS, BASIS, EIGVEC), (2 * BASIS * BLOCKS) ** -0.5, 0.0390625, ((1, 8), (3, 4))),
        "weights": jnp.clip(jnp.exp(math.log(24.0) - 1.3862944 * jax.random.uniform(splits[3], (EIGVEC,), jnp.float32) ** level_of(splits[3], (EIGVEC,), ((0, 4),), -0.2, 0.2)), 6.0, 24.0),
    }


def mix(form, left, right):
    return jnp.einsum(form, left, right, precision=lax.Precision.HIGHEST)


def mix_low(form, left, right):
    return jnp.einsum(form, left.astype(jnp.float32), right.astype(jnp.float32))


def reference(residual, basis, eigvecs, weights):
    res_re, res_im = residual[0], residual[1]
    bas_re, bas_im = basis[0], basis[1]
    eig_re, eig_im = eigvecs[0], eigvecs[1]
    coarse_re = mix("bkc,bnc->bnk", bas_re, res_re) + mix("bkc,bnc->bnk", bas_im, res_im)
    coarse_im = mix("bkc,bnc->bnk", bas_re, res_im) - mix("bkc,bnc->bnk", bas_im, res_re)
    coarse_re = coarse_re.astype(jnp.bfloat16)
    coarse_im = coarse_im.astype(jnp.bfloat16)
    spec_re = mix_low("bnk,bkj->nj", coarse_re, eig_re) + mix_low("bnk,bkj->nj", coarse_im, eig_im)
    spec_im = mix_low("bnk,bkj->nj", coarse_im, eig_re) - mix_low("bnk,bkj->nj", coarse_re, eig_im)
    wgt_re = (spec_re * weights[None, :]).astype(jnp.bfloat16)
    wgt_im = (spec_im * weights[None, :]).astype(jnp.bfloat16)
    lift_re = mix_low("nj,bkj->bnk", wgt_re, eig_re) - mix_low("nj,bkj->bnk", wgt_im, eig_im)
    lift_im = mix_low("nj,bkj->bnk", wgt_re, eig_im) + mix_low("nj,bkj->bnk", wgt_im, eig_re)
    out_re = mix("bkc,bnk->bnc", bas_re, lift_re) - mix("bkc,bnk->bnc", bas_im, lift_im)
    out_im = mix("bkc,bnk->bnc", bas_re, lift_im) + mix("bkc,bnk->bnc", bas_im, lift_re)
    return jnp.stack([out_re, out_im])
```

```python
import functools

import jax
import jax.numpy as jnp
from jax import lax
from jax.experimental import pallas as pl
from jax.experimental.pallas import tpu as pltpu
from jax.sharding import PartitionSpec as P

BF = jnp.bfloat16
F32 = jnp.float32
NT = (((1,), (1,)), ((), ()))
NN = (((1,), (0,)), ((), ()))
MIB = 1 << 20


def dot(left, right, dims):
    return lax.dot_general(left, right, dims, preferred_element_type=F32)


def project_kernel(half, res_ref, bas_ref, out_ref, copy_ref):
    step = pl.program_id(0)
    cols, comp = res_ref.shape[2:]
    pair = 2 * bas_ref.shape[2]
    res = res_ref[...].reshape(4 * cols, comp).astype(BF)
    bas = bas_ref[...].reshape(2 * pair, comp).astype(BF)
    copy_ref[step] = bas
    prod = dot(res, bas, NT)
    first = lax.broadcasted_iota(jnp.int32, (cols, pair), 1) < pair // 2

    def part(row, lane):
        lanes = slice(lane * pair, (lane + 1) * pair)
        top = prod[(2 * row) * cols : (2 * row + 1) * cols, lanes]
        low = prod[(2 * row + 1) * cols : (2 * row + 2) * cols, lanes]
        return jnp.where(first, top, low)

    out_ref[0] = (part(0, 0) + part(1, 1)).astype(out_ref.dtype)
    out_ref[1] = (part(1, 0) - part(0, 1)).astype(out_ref.dtype)


def project(half, residual, basis, dtype):
    _, blocks, cols, comp = residual.shape
    vecs = basis.shape[2]
    pairs = blocks // 4
    where = lambda i, half: (0, half[0] * pairs + i, 0, 0)
    return pl.pallas_call(
        project_kernel,
        grid_spec=pltpu.PrefetchScalarGridSpec(
            num_scalar_prefetch=1,
            grid=(pairs,),
            in_specs=[
                pl.BlockSpec((2, 2, cols, comp), where),
                pl.BlockSpec((2, 2, vecs, comp), where),
            ],
            out_specs=[
                pl.BlockSpec((2, cols, 2 * vecs), lambda i, half: (0, 0, i)),
                pl.BlockSpec(memory_space=pltpu.VMEM),
            ],
        ),
        out_shape=[
            jax.ShapeDtypeStruct((2, cols, pairs * 2 * vecs), dtype),
            pltpu.VMEM((pairs, 4 * vecs, comp), BF),
        ],
        compiler_params=pltpu.CompilerParams(vmem_limit_bytes=16 * MIB),
        cost_estimate=pl.CostEstimate(
            flops=16 * pairs * cols * vecs * comp * 2, bytes_accessed=(residual.size + basis.size) * 2, transcendentals=0
        ),
        name="project",
    )(half, residual, basis)


def contract_kernel(own, own_ref, other_ref, eig_ref, wgt_ref, out_ref):
    cols = own_ref.shape[1]
    depth = own_ref.shape[2]
    re = im = None
    for coarse_ref, half in ((own_ref, own[0]), (other_ref, 1 - own[0])):
        rows = pl.ds(pl.multiple_of(half * depth, depth), depth)
        coarse = coarse_ref[...].reshape(2 * cols, depth)
        by_re = dot(coarse, eig_ref[0, rows, :], NN)
        by_im = dot(coarse, eig_ref[1, rows, :], NN)
        re = by_re[:cols] + by_im[cols:] + (0 if re is None else re)
        im = by_re[cols:] - by_im[:cols] + (0 if im is None else im)
    out_ref[0] = re * wgt_ref[...]
    out_ref[1] = im * wgt_ref[...]


def whole():
    return pl.BlockSpec(memory_space=pltpu.VMEM)


def contract(own, coarse_own, coarse_other, eig, weights):
    _, cols, depth = coarse_own.shape
    vectors = eig.shape[-1]
    return pl.pallas_call(
        contract_kernel,
        in_specs=[pl.BlockSpec(memory_space=pltpu.SMEM)] + [whole()] * 4,
        out_specs=whole(),
        out_shape=jax.ShapeDtypeStruct((2, cols, vectors), F32),
        compiler_params=pltpu.CompilerParams(vmem_limit_bytes=16 * MIB),
        cost_estimate=pl.CostEstimate(flops=16 * cols * depth * vectors, bytes_accessed=eig.size * 2, transcendentals=0),
        name="contract",
    )(own, coarse_own, coarse_other, eig, weights)


def expand_kernel(half, wgt_ref, eig_ref, out_ref):
    cols, depth = out_ref.shape[1:]
    rows = pl.ds(pl.multiple_of(half[0] * depth, depth), depth)
    weighted = wgt_ref[...].reshape(2 * cols, wgt_ref.shape[2])
    by_re = dot(weighted, eig_ref[0, rows, :], NT)
    by_im = dot(weighted, eig_ref[1, rows, :], NT)
    out_ref[0] = (by_re[:cols] - by_im[cols:]).astype(out_ref.dtype)
    out_ref[1] = (by_re[cols:] + by_im[:cols]).astype(out_ref.dtype)


def expand(half, weighted, eig, dtype):
    _, cols, vectors = weighted.shape
    depth = eig.shape[1] // 2
    return pl.pallas_call(
        expand_kernel,
        in_specs=[pl.BlockSpec(memory_space=pltpu.SMEM)] + [whole()] * 2,
        out_specs=whole(),
        out_shape=jax.ShapeDtypeStruct((2, cols, depth), dtype),
        compiler_params=pltpu.CompilerParams(vmem_limit_bytes=16 * MIB),
        cost_estimate=pl.CostEstimate(flops=8 * cols * depth * vectors, bytes_accessed=eig.size, transcendentals=0),
        name="expand",
    )(half, weighted, eig)


def prolong_kernel(half, lift_ref, bas_ref, *refs):
    out_ref = refs[-1]
    step = pl.program_id(0)
    cols, comp = out_ref.shape[2:]
    pair = bas_ref.shape[1] // 2
    re, im = lift_ref[0], lift_ref[1]
    first = lax.broadcasted_iota(jnp.int32, (cols, pair), 1) < pair // 2
    none = jnp.zeros_like(re)
    re0, re1 = jnp.where(first, re, none), jnp.where(first, none, re)
    im0, im1 = jnp.where(first, im, none), jnp.where(first, none, im)
    left = jnp.concatenate(
        [
            jnp.concatenate([re0, re1, im0, im1], axis=0),
            jnp.concatenate([-im0, -im1, re0, re1], axis=0),
        ],
        axis=1,
    )
    out_ref[...] = dot(left, bas_ref[step], NN).reshape(out_ref.shape)


def prolong(half, lifted, bas, shape, into=None):
    _, cols, depth = lifted.shape
    pairs, rows, comp = bas.shape
    where = lambda i, half: (0, half[0] * pairs + i, 0, 0)
    out = jax.ShapeDtypeStruct(shape, F32)
    return pl.pallas_call(
        prolong_kernel,
        grid_spec=pltpu.PrefetchScalarGridSpec(
            num_scalar_prefetch=1,
            grid=(pairs,),
            in_specs=[
                pl.BlockSpec((2, cols, rows // 2), lambda i, half: (0, 0, i)),
                pl.BlockSpec(memory_space=pltpu.VMEM),
            ]
            + ([] if into is None else [pl.BlockSpec(memory_space=pl.ANY)]),
            out_specs=pl.BlockSpec((2, 2, cols, comp), where),
        ),
        out_shape=out,
        input_output_aliases={} if into is None else {3: 0},
        compiler_params=pltpu.CompilerParams(vmem_limit_bytes=16 * MIB),
        cost_estimate=pl.CostEstimate(flops=4 * cols * 2 * depth * comp * 2, bytes_accessed=2 * cols * depth // 8 * comp, transcendentals=0),
        name="prolong",
    )(half, lifted, bas, *(() if into is None else (into,)))


def swap(value, axis, size, step):
    return lax.ppermute(value, axis, [(i, i ^ step) for i in range(size)])


def sum_chips(value, size):
    step = 2
    while step < size:
        value = (value.astype(F32) + swap(value.astype(BF), "eig", size, step).astype(F32)).astype(BF)
        step *= 2
    return value


def sum_regions(value, size):
    step = 1
    while step < size:
        steps = [step] if step == 1 or 2 * step >= size else [step, 2 * step, 3 * step]
        sent = value.astype(BF)
        for arrived in [swap(sent, "region", size, s) for s in steps]:
            value = value + arrived.astype(F32)
        step *= 2 if len(steps) == 1 else 4
    return value


def shards(regions, shares, residual, basis, eigvecs, weights):
    own = (lax.axis_index("eig") % 2).astype(jnp.int32).reshape(1)
    other = 1 - own
    blocks, vecs = basis.shape[1:3]
    eig = eigvecs.reshape(2, blocks * vecs, eigvecs.shape[3])

    part_other, bas_other = project(other, residual, basis, BF)
    got = swap(part_other, "eig", shares, 1)
    part_own, bas_own = project(own, residual, basis, F32)
    coarse_own = sum_chips((part_own + got.astype(F32)).astype(BF), shares)
    coarse_other = swap(coarse_own, "eig", shares, 1)

    spectral = contract(own, coarse_own, coarse_other, eig, weights.reshape(1, -1))
    weighted = sum_regions(spectral, regions).astype(BF)

    lift_other = expand(other, weighted, eig, BF)
    got = swap(lift_other, "eig", shares, 1)
    lift_own = expand(own, weighted, eig, F32)
    lifted_own = sum_chips((lift_own + got.astype(F32)).astype(BF), shares)
    lifted_other = swap(lifted_own, "eig", shares, 1)

    out = prolong(own, lifted_own, bas_own, residual.shape)
    return prolong(other, lifted_other, bas_other, residual.shape, out)


def solution(mesh):
    split = P(None, "region", None, "eig")
    return jax.shard_map(
        functools.partial(shards, mesh.shape["region"], mesh.shape["eig"]),
        mesh=mesh,
        in_specs=(split, split, split, P("eig")),
        out_specs=split,
        check_vma=False,
    )
```

```python
import functools

import jax
import jax.numpy as jnp
from jax import lax
from jax.experimental import pallas as pl
from jax.experimental.pallas import tpu as pltpu
from jax.sharding import PartitionSpec as P

BF = jnp.bfloat16
F32 = jnp.float32
NT = (((1,), (1,)), ((), ()))
NN = (((1,), (0,)), ((), ()))
MIB = 1 << 20


def dot(left, right, dims):
    return lax.dot_general(left, right, dims, preferred_element_type=F32)


def project_kernel(own, res_hbm, bas_hbm, other_ref, own_ref, bas_other_ref, bas_own_ref, res_ref, bas_ref, sem):
    cols, comp = res_ref.shape[2:]
    vecs = bas_ref.shape[2]
    pair = 2 * vecs
    pairs = bas_own_ref.shape[0]

    def copies(i):
        half = 1 - own[0] if i < pairs else own[0]
        source = pl.ds(2 * (half * pairs + i % pairs), 2)
        slot = pl.ds(2 * i, 2)
        return (
            pltpu.make_async_copy(res_hbm.at[:, source], res_ref.at[:, slot], sem.at[0, i]),
            pltpu.make_async_copy(bas_hbm.at[:, source], bas_ref.at[:, slot], sem.at[1, i]),
        )

    for i in range(2 * pairs):
        for copy in copies(i):
            copy.start()
    first = lax.broadcasted_iota(jnp.int32, (cols, pair), 1) < vecs
    for i in range(2 * pairs):
        out_ref, copy_ref = (other_ref, bas_other_ref) if i < pairs else (own_ref, bas_own_ref)
        for copy in copies(i):
            copy.wait()
        res = res_ref[:, 2 * i : 2 * i + 2].reshape(4 * cols, comp).astype(BF)
        bas = bas_ref[:, 2 * i : 2 * i + 2].reshape(2 * pair, comp).astype(BF)
        copy_ref[i % pairs] = bas
        prod = dot(res, bas, NT)

        def part(row, lane):
            lanes = slice(lane * pair, (lane + 1) * pair)
            top = prod[2 * row * cols : (2 * row + 1) * cols, lanes]
            low = prod[(2 * row + 1) * cols : (2 * row + 2) * cols, lanes]
            return jnp.where(first, top, low)

        lanes = slice(i % pairs * pair, (i % pairs + 1) * pair)
        out_ref[0, :, lanes] = (part(0, 0) + part(1, 1)).astype(out_ref.dtype)
        out_ref[1, :, lanes] = (part(1, 0) - part(0, 1)).astype(out_ref.dtype)


def hbm(value):
    return pltpu.with_memory_space_constraint(value, pltpu.HBM)


def project(own, residual, basis):
    _, blocks, cols, comp = residual.shape
    vecs = basis.shape[2]
    pairs = blocks // 4
    return pl.pallas_call(
        project_kernel,
        in_specs=[pl.BlockSpec(memory_space=pltpu.SMEM)] + [pl.BlockSpec(memory_space=pltpu.HBM)] * 2,
        out_specs=[whole()] * 4,
        out_shape=[
            pltpu.VMEM((2, cols, pairs * 2 * vecs), BF),
            pltpu.VMEM((2, cols, pairs * 2 * vecs), F32),
            pltpu.VMEM((pairs, 4 * vecs, comp), BF),
            pltpu.VMEM((pairs, 4 * vecs, comp), BF),
        ],
        scratch_shapes=[
            pltpu.VMEM(residual.shape, F32),
            pltpu.VMEM(basis.shape, F32),
            pltpu.SemaphoreType.DMA((2, 2 * pairs)),
        ],
        compiler_params=pltpu.CompilerParams(vmem_limit_bytes=28 * MIB),
        cost_estimate=pl.CostEstimate(
            flops=16 * blocks * cols * vecs * comp, bytes_accessed=(residual.size + basis.size) * 4, transcendentals=0
        ),
        name="project",
    )(own, hbm(residual), hbm(basis))


def contract_kernel(own, own_ref, other_ref, eig_ref, wgt_ref, out_ref):
    cols = own_ref.shape[1]
    depth = own_ref.shape[2]
    re = im = None
    for coarse_ref, half in ((own_ref, own[0]), (other_ref, 1 - own[0])):
        rows = pl.ds(pl.multiple_of(half * depth, depth), depth)
        coarse = coarse_ref[...].reshape(2 * cols, depth)
        by_re = dot(coarse, eig_ref[0, rows, :], NN)
        by_im = dot(coarse, eig_ref[1, rows, :], NN)
        re = by_re[:cols] + by_im[cols:] + (0 if re is None else re)
        im = by_re[cols:] - by_im[:cols] + (0 if im is None else im)
    out_ref[0] = re * wgt_ref[...]
    out_ref[1] = im * wgt_ref[...]


def whole():
    return pl.BlockSpec(memory_space=pltpu.VMEM)


def contract(own, coarse_own, coarse_other, eig, weights):
    _, cols, depth = coarse_own.shape
    vectors = eig.shape[-1]
    return pl.pallas_call(
        contract_kernel,
        in_specs=[pl.BlockSpec(memory_space=pltpu.SMEM)] + [whole()] * 4,
        out_specs=whole(),
        out_shape=jax.ShapeDtypeStruct((2, cols, vectors), F32),
        compiler_params=pltpu.CompilerParams(vmem_limit_bytes=16 * MIB),
        cost_estimate=pl.CostEstimate(flops=16 * cols * depth * vectors, bytes_accessed=eig.size * 2, transcendentals=0),
        name="contract",
    )(own, coarse_own, coarse_other, eig, weights)


def expand_kernel(half, wgt_ref, eig_ref, out_ref):
    cols, depth = out_ref.shape[1:]
    rows = pl.ds(pl.multiple_of(half[0] * depth, depth), depth)
    weighted = wgt_ref[...].reshape(2 * cols, wgt_ref.shape[2])
    by_re = dot(weighted, eig_ref[0, rows, :], NT)
    by_im = dot(weighted, eig_ref[1, rows, :], NT)
    out_ref[0] = (by_re[:cols] - by_im[cols:]).astype(out_ref.dtype)
    out_ref[1] = (by_re[cols:] + by_im[:cols]).astype(out_ref.dtype)


def expand(half, weighted, eig, dtype):
    _, cols, vectors = weighted.shape
    depth = eig.shape[1] // 2
    return pl.pallas_call(
        expand_kernel,
        in_specs=[pl.BlockSpec(memory_space=pltpu.SMEM)] + [whole()] * 2,
        out_specs=whole(),
        out_shape=jax.ShapeDtypeStruct((2, cols, depth), dtype),
        compiler_params=pltpu.CompilerParams(vmem_limit_bytes=16 * MIB),
        cost_estimate=pl.CostEstimate(flops=8 * cols * depth * vectors, bytes_accessed=eig.size, transcendentals=0),
        name="expand",
    )(half, weighted, eig)


def prolong_kernel(half, lift_ref, bas_ref, *refs):
    out_hbm, out_ref, sem = refs[-3:]
    cols, comp = out_ref.shape[2:]
    pairs, pair = bas_ref.shape[0], bas_ref.shape[1] // 2
    first = lax.broadcasted_iota(jnp.int32, (cols, pair), 1) < pair // 2

    def copy(i):
        target = pl.ds(2 * (half[0] * pairs + i), 2)
        return pltpu.make_async_copy(out_ref.at[:, pl.ds(2 * i, 2)], out_hbm.at[:, target], sem.at[i])

    for i in range(pairs):
        lanes = slice(i * pair, (i + 1) * pair)
        re, im = lift_ref[0, :, lanes], lift_ref[1, :, lanes]
        none = jnp.zeros_like(re)
        re0, re1 = jnp.where(first, re, none), jnp.where(first, none, re)
        im0, im1 = jnp.where(first, im, none), jnp.where(first, none, im)
        left = jnp.concatenate(
            [
                jnp.concatenate([re0, re1, im0, im1], axis=0),
                jnp.concatenate([-im0, -im1, re0, re1], axis=0),
            ],
            axis=1,
        )
        out_ref[:, 2 * i : 2 * i + 2] = dot(left, bas_ref[i], NN).reshape(2, 2, cols, comp)
        copy(i).start()
    for i in range(pairs):
        copy(i).wait()


def prolong(half, lifted, bas, shape, into=None):
    _, cols, depth = lifted.shape
    pairs, rows, comp = bas.shape
    anywhere = pl.BlockSpec(memory_space=pltpu.HBM)
    return pl.pallas_call(
        prolong_kernel,
        in_specs=[pl.BlockSpec(memory_space=pltpu.SMEM)] + [whole()] * 2 + ([] if into is None else [anywhere]),
        out_specs=anywhere,
        out_shape=jax.ShapeDtypeStruct(shape, F32),
        input_output_aliases={} if into is None else {3: 0},
        scratch_shapes=[pltpu.VMEM((2, 2 * pairs, cols, comp), F32), pltpu.SemaphoreType.DMA((pairs,))],
        compiler_params=pltpu.CompilerParams(vmem_limit_bytes=16 * MIB),
        cost_estimate=pl.CostEstimate(flops=16 * pairs * cols * rows * comp, bytes_accessed=pairs * cols * comp * 16, transcendentals=0),
        name="prolong",
    )(half, lifted, bas, *(() if into is None else (into,)))


def swap(value, axis, size, step):
    return lax.ppermute(value, axis, [(i, i ^ step) for i in range(size)])


def sum_chips(value, size):
    step = 2
    while step < size:
        value = (value.astype(F32) + swap(value.astype(BF), "eig", size, step).astype(F32)).astype(BF)
        step *= 2
    return value


def sum_regions(value, size):
    step = 1
    while step < size:
        steps = [step] if step == 1 or 2 * step >= size else [step, 2 * step, 3 * step]
        sent = value.astype(BF)
        for arrived in [swap(sent, "region", size, s) for s in steps]:
            value = value + arrived.astype(F32)
        step *= 2 if len(steps) == 1 else 4
    return value


def shards(regions, shares, residual, basis, eigvecs, weights):
    own = (lax.axis_index("eig") % 2).astype(jnp.int32).reshape(1)
    other = 1 - own
    blocks, vecs = basis.shape[1:3]
    eig = eigvecs.reshape(2, blocks * vecs, eigvecs.shape[3])

    part_other, part_own, bas_other, bas_own = project(own, residual, basis)
    got = swap(part_other, "eig", shares, 1)
    coarse_own = sum_chips((part_own + got.astype(F32)).astype(BF), shares)
    coarse_other = swap(coarse_own, "eig", shares, 1)

    spectral = contract(own, coarse_own, coarse_other, eig, weights.reshape(1, -1))
    weighted = sum_regions(spectral, regions).astype(BF)

    lift_other = expand(other, weighted, eig, BF)
    got = swap(lift_other, "eig", shares, 1)
    lift_own = expand(own, weighted, eig, F32)
    lifted_own = sum_chips((lift_own + got.astype(F32)).astype(BF), shares)
    lifted_other = swap(lifted_own, "eig", shares, 1)

    out = prolong(own, lifted_own, bas_own, residual.shape)
    return prolong(other, lifted_other, bas_other, residual.shape, out)


def solution(mesh):
    split = P(None, "region", None, "eig")
    return jax.shard_map(
        functools.partial(shards, mesh.shape["region"], mesh.shape["eig"]),
        mesh=mesh,
        in_specs=(split, split, split, P("eig")),
        out_specs=split,
        check_vma=False,
    )
```

```python
import functools

import jax
import jax.numpy as jnp
from jax import lax
from jax.experimental import pallas as pl
from jax.experimental.pallas import tpu as pltpu
from jax.sharding import PartitionSpec as P

BF = jnp.bfloat16
F32 = jnp.float32
NT = (((1,), (1,)), ((), ()))
NN = (((1,), (0,)), ((), ()))
MIB = 1 << 20


def dot(left, right, dims):
    return lax.dot_general(left, right, dims, preferred_element_type=F32)


def project_kernel(res_hbm, bas_hbm, sent_ref, res_ref, bas_ref, sem):
    cols, comp = res_ref.shape[2:]
    vecs = bas_ref.shape[2]
    pair = 2 * vecs
    pairs = sem.shape[1]

    def copies(i):
        two = pl.ds(2 * i, 2)
        return (
            pltpu.make_async_copy(res_hbm.at[:, two], res_ref.at[:, two], sem.at[0, i]),
            pltpu.make_async_copy(bas_hbm.at[:, two], bas_ref.at[:, two], sem.at[1, i]),
        )

    for i in range(pairs):
        for copy in copies(i):
            copy.start()
    first = lax.broadcasted_iota(jnp.int32, (cols, pair), 1) < vecs
    for i in range(pairs):
        for copy in copies(i):
            copy.wait()
        res = res_ref[:, 2 * i : 2 * i + 2].reshape(4 * cols, comp).astype(BF)
        bas = bas_ref[:, 2 * i : 2 * i + 2].reshape(2 * pair, comp).astype(BF)
        prod = dot(res, bas, NT)

        def part(row, lane):
            lanes = slice(lane * pair, (lane + 1) * pair)
            top = prod[2 * row * cols : (2 * row + 1) * cols, lanes]
            low = prod[(2 * row + 1) * cols : (2 * row + 2) * cols, lanes]
            return jnp.where(first, top, low)

        lanes = slice(i * pair, (i + 1) * pair)
        re, im = part(0, 0) + part(1, 1), part(1, 0) - part(0, 1)
        for row, value in ((0, re), (1, im)):
            sent_ref[row, :, lanes] = value.astype(BF)


def hbm(value):
    return pltpu.with_memory_space_constraint(value, pltpu.HBM)


def whole():
    return pl.BlockSpec(memory_space=pltpu.VMEM)


def scalar():
    return pl.BlockSpec(memory_space=pltpu.SMEM)


def project(residual, basis):
    _, blocks, cols, comp = residual.shape
    vecs = basis.shape[2]
    return pl.pallas_call(
        project_kernel,
        in_specs=[pl.BlockSpec(memory_space=pltpu.HBM)] * 2,
        out_specs=whole(),
        out_shape=jax.ShapeDtypeStruct((2, cols, blocks * vecs), BF),
        scratch_shapes=[
            pltpu.VMEM(residual.shape, F32),
            pltpu.VMEM(basis.shape, F32),
            pltpu.SemaphoreType.DMA((2, blocks // 2)),
        ],
        compiler_params=pltpu.CompilerParams(vmem_limit_bytes=18 * MIB),
        cost_estimate=pl.CostEstimate(
            flops=16 * blocks * cols * vecs * comp, bytes_accessed=(residual.size + basis.size) * 4, transcendentals=0
        ),
        name="project",
    )(hbm(residual), hbm(basis))


def contract_kernel(active, own_ref, sister_ref, wgt_ref, *refs):
    *coarse_refs, out_ref = refs
    cols, depth = coarse_refs[0].shape[1:]
    count = own_ref.shape[2]

    @pl.when(active[0] == 1)
    def _():
        coarse = total([ref[...] for ref in coarse_refs]).astype(BF).reshape(2 * cols, depth)
        for i, eig_ref in enumerate((own_ref, sister_ref)):
            by_re = dot(coarse, eig_ref[0], NN)
            by_im = dot(coarse, eig_ref[1], NN)
            re = by_re[:cols] + by_im[cols:]
            im = by_re[cols:] - by_im[:cols]
            if i == 0:
                re, im = re * wgt_ref[...], im * wgt_ref[...]
            out_ref[0, :, i * count : (i + 1) * count] = re.astype(BF)
            out_ref[1, :, i * count : (i + 1) * count] = im.astype(BF)


def contract(active, coarse, own, sister, weights):
    _, cols, depth = coarse[0].shape
    count = own.shape[2]
    return pl.pallas_call(
        contract_kernel,
        in_specs=[scalar()] + [whole()] * 3 + [whole()] * len(coarse),
        out_specs=whole(),
        out_shape=jax.ShapeDtypeStruct((2, cols, 2 * count), BF),
        compiler_params=pltpu.CompilerParams(vmem_limit_bytes=4 * MIB),
        cost_estimate=pl.CostEstimate(flops=16 * cols * depth * count, bytes_accessed=own.size * 4, transcendentals=0),
        name="contract",
    )(active, own, sister, weights, *coarse)


def expand_kernel(own_first, active, own_ref, sister_ref, *refs):
    *wgt_refs, out_ref = refs
    cols = out_ref.shape[1]
    count = own_ref.shape[2]

    @pl.when(active[0] == 1)
    def _():
        whole_wgt = total([ref[...] for ref in wgt_refs]).astype(BF)
        re = im = None
        for i, eig_ref in enumerate((own_ref, sister_ref) if own_first else (sister_ref, own_ref)):
            weighted = whole_wgt[:, :, i * count : (i + 1) * count].reshape(2 * cols, count)
            by_re = dot(weighted, eig_ref[0], NT)
            by_im = dot(weighted, eig_ref[1], NT)
            re = by_re[:cols] - by_im[cols:] + (0 if re is None else re)
            im = by_re[cols:] + by_im[:cols] + (0 if im is None else im)
        out_ref[0] = re.astype(BF)
        out_ref[1] = im.astype(BF)


def expand(active, weighted, own, sister, own_first):
    cols = weighted[0].shape[1]
    depth, count = own.shape[1:]
    return pl.pallas_call(
        functools.partial(expand_kernel, own_first),
        in_specs=[scalar()] + [whole()] * 2 + [whole()] * len(weighted),
        out_specs=whole(),
        out_shape=jax.ShapeDtypeStruct((2, cols, depth), BF),
        compiler_params=pltpu.CompilerParams(vmem_limit_bytes=4 * MIB),
        cost_estimate=pl.CostEstimate(flops=16 * cols * depth * count, bytes_accessed=own.size * 4, transcendentals=0),
        name="expand",
    )(active, own, sister, *weighted)


def load_kernel(from_hbm, to_ref, sem):
    copy = pltpu.make_async_copy(from_hbm, to_ref, sem)
    copy.start()
    copy.wait()


def load(value):
    return pl.pallas_call(
        load_kernel,
        in_specs=[pl.BlockSpec(memory_space=pltpu.HBM)],
        out_specs=whole(),
        out_shape=pltpu.VMEM(value.shape, value.dtype),
        scratch_shapes=[pltpu.SemaphoreType.DMA],
        compiler_params=pltpu.CompilerParams(vmem_limit_bytes=4 * MIB),
        cost_estimate=pl.CostEstimate(flops=0, bytes_accessed=value.size * 4, transcendentals=0),
        name="load",
    )(hbm(value))


def prolong_kernel(active, sum_ref, arrived_ref, bas_ref, out_hbm, out_ref, sem):
    cols, comp = out_ref.shape[2:]
    pair = 2 * bas_ref.shape[2]
    pairs = sem.shape[0]
    first = lax.broadcasted_iota(jnp.int32, (cols, pair), 1) < pair // 2

    def copy(i):
        two = pl.ds(2 * i, 2)
        return pltpu.make_async_copy(out_ref.at[:, two], out_hbm.at[:, two], sem.at[i])

    for i in range(pairs):
        lanes = slice(i * pair, (i + 1) * pair)
        re, im = (jnp.where(active[0] == 1, arrived_ref[row, :, lanes], sum_ref[row, :, lanes]) for row in range(2))
        none = jnp.zeros_like(re)
        re0, re1 = jnp.where(first, re, none), jnp.where(first, none, re)
        im0, im1 = jnp.where(first, im, none), jnp.where(first, none, im)
        left = jnp.concatenate(
            [
                jnp.concatenate([re0, re1, im0, im1], axis=0),
                jnp.concatenate([-im0, -im1, re0, re1], axis=0),
            ],
            axis=1,
        )
        bas = bas_ref[:, 2 * i : 2 * i + 2].reshape(2 * pair, comp).astype(BF)
        out_ref[:, 2 * i : 2 * i + 2] = dot(left, bas, NN).reshape(2, 2, cols, comp)
        copy(i).start()
    for i in range(pairs):
        copy(i).wait()


def prolong(active, lifted, arrived, basis, shape):
    vecs, comp = basis.shape[2:]
    cols = lifted.shape[1]
    pairs = shape[1] // 2
    return pl.pallas_call(
        prolong_kernel,
        in_specs=[scalar()] + [whole()] * 3,
        out_specs=pl.BlockSpec(memory_space=pltpu.HBM),
        out_shape=jax.ShapeDtypeStruct(shape, F32),
        scratch_shapes=[pltpu.VMEM(shape, F32), pltpu.SemaphoreType.DMA((pairs,))],
        compiler_params=pltpu.CompilerParams(vmem_limit_bytes=8 * MIB),
        cost_estimate=pl.CostEstimate(flops=64 * pairs * cols * vecs * comp, bytes_accessed=pairs * cols * comp * 16, transcendentals=0),
        name="prolong",
    )(active, lifted, arrived, basis)


class Slice:
    def __init__(self, regions, shares):
        self.regions, self.shares = regions, shares

    def swap(self, value):
        return lax.ppermute(value, "eig", [(i, i ^ 1) for i in range(self.shares)])

    def cross(self, value, sender, region=0, chip=0):
        pairs = []
        for i in range(self.regions * self.shares):
            far = (i ^ (region * self.shares) ^ (2 * chip)) ^ 1
            pairs.append((i, far if i % 2 == sender else i ^ 1))
        return lax.ppermute(value, ("region", "eig"), pairs)

    def region_steps(self):
        step = 1
        while step < self.regions:
            four = step > 1 and 2 * step < self.regions
            yield [step, 2 * step, 3 * step] if four else [step]
            step *= 4 if four else 2

    def chip_steps(self):
        return range(1, self.shares // 2)


def total(terms):
    value = terms[0].astype(F32)
    for term in terms[1:]:
        value = value + term.astype(F32)
    return value


def add_kernel(scale_ref, *refs):
    *term_refs, out_ref = refs
    value = total([ref[...] for ref in term_refs])
    half = out_ref.shape[2] // 2
    if scale_ref is None:
        out_ref[...] = value.astype(BF)
    else:
        out_ref[:, :, :half] = value[:, :, :half].astype(BF)
        out_ref[:, :, half:] = (value[:, :, half:] * scale_ref[...]).astype(BF)


def add(terms, scale=None):
    kernel = functools.partial(add_kernel, None) if scale is None else add_kernel
    return pl.pallas_call(
        kernel,
        in_specs=([] if scale is None else [whole()]) + [whole()] * len(terms),
        out_specs=whole(),
        out_shape=jax.ShapeDtypeStruct(terms[0].shape, BF),
        compiler_params=pltpu.CompilerParams(vmem_limit_bytes=4 * MIB),
        cost_estimate=pl.CostEstimate(flops=terms[0].size * 2, bytes_accessed=terms[0].size * 4, transcendentals=0),
        name="add",
    )(*([] if scale is None else [scale]), *terms)


def shards(regions, shares, residual, basis, eigvecs, weights):
    place = Slice(regions, shares)
    core = (lax.axis_index("eig") % 2).astype(jnp.int32).reshape(1)
    blocks, vecs = basis.shape[1:3]
    count = eigvecs.shape[3]
    own = eigvecs.reshape(2, blocks * vecs, count)
    weights = weights.reshape(1, 1, count)

    part = project(residual, basis)
    chip_sum = add([part, place.swap(part)])
    sister = place.swap(lax.optimization_barrier((own, chip_sum))[0])
    holder = 1
    coarse = [chip_sum] + [place.cross(chip_sum, 0, chip=s) for s in place.chip_steps()]

    start = holder
    active = (core == holder).astype(jnp.int32)
    value = contract(active, coarse, own, sister, weights.reshape(1, count))
    steps = list(place.region_steps())
    for i, step in enumerate(steps):
        terms = [place.swap(value)] + [place.cross(value, holder, region=s) for s in step]
        holder = 1 - holder
        if i < len(steps) - 1:
            value = add(terms, weights if i == 0 else None)

    active = (core == holder).astype(jnp.int32)
    lifted = expand(active, terms, own, sister, holder == start)
    in_vmem = load(lax.optimization_barrier((basis, lifted))[0])
    terms = [place.swap(lifted)] + [place.cross(lifted, holder, chip=s) for s in place.chip_steps()]
    terms, in_vmem = lax.optimization_barrier((terms, in_vmem))
    lifted = add(terms)
    return prolong(active, lifted, place.swap(lifted), in_vmem, residual.shape)


def solution(mesh):
    split = P(None, "region", None, "eig")
    return jax.shard_map(
        functools.partial(shards, mesh.shape["region"], mesh.shape["eig"]),
        mesh=mesh,
        in_specs=(split, split, split, P("eig")),
        out_specs=split,
        check_vma=False,
    )
```

```python
import functools
import math

import jax
import jax.numpy as jnp
from jax import lax
from jax.experimental import pallas as pl
from jax.experimental.pallas import tpu as pltpu
from jax.sharding import PartitionSpec as P

BF = jnp.bfloat16
F32 = jnp.float32
NT = (((1,), (1,)), ((), ()))
NN = (((1,), (0,)), ((), ()))
MIB = 1 << 20


def dot(left, right, dims):
    return lax.dot_general(left, right, dims, preferred_element_type=F32)


def project_kernel(res_hbm, bas_hbm, sent_ref, res_ref, bas_ref, sem):
    cols, comp = res_ref.shape[2:]
    vecs = bas_ref.shape[2]
    pair = 2 * vecs
    pairs = sem.shape[1]

    def copies(i):
        two = pl.ds(2 * i, 2)
        return (
            pltpu.make_async_copy(res_hbm.at[:, two], res_ref.at[:, two], sem.at[0, i]),
            pltpu.make_async_copy(bas_hbm.at[:, two], bas_ref.at[:, two], sem.at[1, i]),
        )

    for i in range(pairs):
        for copy in copies(i):
            copy.start()
    first = lax.broadcasted_iota(jnp.int32, (cols, pair), 1) < vecs
    for i in range(pairs):
        for copy in copies(i):
            copy.wait()
        res = res_ref[:, 2 * i : 2 * i + 2].reshape(4 * cols, comp).astype(BF)
        bas = bas_ref[:, 2 * i : 2 * i + 2].reshape(2 * pair, comp).astype(BF)
        prod = dot(res, bas, NT)

        def part(row, lane):
            lanes = slice(lane * pair, (lane + 1) * pair)
            top = prod[2 * row * cols : (2 * row + 1) * cols, lanes]
            low = prod[(2 * row + 1) * cols : (2 * row + 2) * cols, lanes]
            return jnp.where(first, top, low)

        lanes = slice(i * pair, (i + 1) * pair)
        re, im = part(0, 0) + part(1, 1), part(1, 0) - part(0, 1)
        for row, value in ((0, re), (1, im)):
            sent_ref[row, :, lanes] = value.astype(BF)


def hbm(value):
    return pltpu.with_memory_space_constraint(value, pltpu.HBM)


def whole():
    return pl.BlockSpec(memory_space=pltpu.VMEM)


def scalar():
    return pl.BlockSpec(memory_space=pltpu.SMEM)


def project(residual, basis):
    _, blocks, cols, comp = residual.shape
    vecs = basis.shape[2]
    return pl.pallas_call(
        project_kernel,
        in_specs=[pl.BlockSpec(memory_space=pltpu.HBM)] * 2,
        out_specs=whole(),
        out_shape=jax.ShapeDtypeStruct((2, cols, blocks * vecs), BF),
        scratch_shapes=[
            pltpu.VMEM(residual.shape, F32),
            pltpu.VMEM(basis.shape, F32),
            pltpu.SemaphoreType.DMA((2, blocks // 2)),
        ],
        compiler_params=pltpu.CompilerParams(vmem_limit_bytes=18 * MIB),
        cost_estimate=pl.CostEstimate(
            flops=16 * blocks * cols * vecs * comp, bytes_accessed=(residual.size + basis.size) * 4, transcendentals=0
        ),
        name="project",
    )(hbm(residual), hbm(basis))


def contract_kernel(active, own_ref, sister_ref, wgt_ref, *refs):
    *coarse_refs, out_ref = refs
    cols, depth = coarse_refs[0].shape[1:]
    count = own_ref.shape[2]

    @pl.when(active[0] == 1)
    def _():
        coarse = total([ref[...] for ref in coarse_refs]).astype(BF).reshape(2 * cols, depth)
        for i, eig_ref in enumerate((own_ref, sister_ref)):
            by_re = dot(coarse, eig_ref[0], NN)
            by_im = dot(coarse, eig_ref[1], NN)
            re = by_re[:cols] + by_im[cols:]
            im = by_re[cols:] - by_im[:cols]
            if i == 0:
                re, im = re * wgt_ref[...], im * wgt_ref[...]
            out_ref[0, :, i * count : (i + 1) * count] = re.astype(BF)
            out_ref[1, :, i * count : (i + 1) * count] = im.astype(BF)


def contract(active, coarse, own, sister, weights):
    _, cols, depth = coarse[0].shape
    count = own.shape[2]
    return pl.pallas_call(
        contract_kernel,
        in_specs=[scalar()] + [whole()] * 3 + [whole()] * len(coarse),
        out_specs=whole(),
        out_shape=jax.ShapeDtypeStruct((2, cols, 2 * count), BF),
        compiler_params=pltpu.CompilerParams(vmem_limit_bytes=4 * MIB),
        cost_estimate=pl.CostEstimate(flops=16 * cols * depth * count, bytes_accessed=own.size * 4, transcendentals=0),
        name="contract",
    )(active, own, sister, weights, *coarse)


def expand_kernel(own_first, active, own_ref, sister_ref, *refs):
    *wgt_refs, out_ref = refs
    cols = out_ref.shape[1]
    count = own_ref.shape[2]

    @pl.when(active[0] == 1)
    def _():
        whole_wgt = total([ref[...] for ref in wgt_refs]).astype(BF)
        re = im = None
        for i, eig_ref in enumerate((own_ref, sister_ref) if own_first else (sister_ref, own_ref)):
            weighted = whole_wgt[:, :, i * count : (i + 1) * count].reshape(2 * cols, count)
            by_re = dot(weighted, eig_ref[0], NT)
            by_im = dot(weighted, eig_ref[1], NT)
            re = by_re[:cols] - by_im[cols:] + (0 if re is None else re)
            im = by_re[cols:] + by_im[:cols] + (0 if im is None else im)
        out_ref[0] = re.astype(BF)
        out_ref[1] = im.astype(BF)


def expand(active, weighted, own, sister, own_first):
    cols = weighted[0].shape[1]
    depth, count = own.shape[1:]
    return pl.pallas_call(
        functools.partial(expand_kernel, own_first),
        in_specs=[scalar()] + [whole()] * 2 + [whole()] * len(weighted),
        out_specs=whole(),
        out_shape=jax.ShapeDtypeStruct((2, cols, depth), BF),
        compiler_params=pltpu.CompilerParams(vmem_limit_bytes=4 * MIB),
        cost_estimate=pl.CostEstimate(flops=16 * cols * depth * count, bytes_accessed=own.size * 4, transcendentals=0),
        name="expand",
    )(active, own, sister, *weighted)


def load_kernel(start, from_hbm, to_ref, sem):
    copy = pltpu.make_async_copy(from_hbm.at[:, pl.ds(start, to_ref.shape[1])], to_ref, sem)
    copy.start()
    copy.wait()


def load(value, start, size, after):
    shape = value.shape[:1] + (size,) + value.shape[2:]
    return pl.pallas_call(
        functools.partial(load_kernel, start),
        in_specs=[pl.BlockSpec(memory_space=pltpu.HBM)],
        out_specs=whole(),
        out_shape=pltpu.VMEM(shape, value.dtype),
        scratch_shapes=[pltpu.SemaphoreType.DMA],
        compiler_params=pltpu.CompilerParams(vmem_limit_bytes=4 * MIB),
        cost_estimate=pl.CostEstimate(flops=0, bytes_accessed=math.prod(shape) * 4, transcendentals=0),
        name="load",
    )(hbm(lax.optimization_barrier((value, after))[0]))


def prolong_kernel(here_ref, there_ref, *refs):
    *bas_refs, out_hbm, out_ref, sem = refs
    cols, comp = out_ref.shape[2:]
    pair = 2 * bas_refs[0].shape[2]
    pairs = sem.shape[0]
    head = bas_refs[0].shape[1] // 2
    first = lax.broadcasted_iota(jnp.int32, (cols, pair), 1) < pair // 2

    def copy(i):
        two = pl.ds(2 * i, 2)
        return pltpu.make_async_copy(out_ref.at[:, two], out_hbm.at[:, two], sem.at[i])

    for i in range(pairs):
        lanes = slice(i * pair, (i + 1) * pair)
        re, im = (total([ref[row, :, lanes] for ref in (here_ref, there_ref)]).astype(BF) for row in range(2))
        none = jnp.zeros_like(re)
        re0, re1 = jnp.where(first, re, none), jnp.where(first, none, re)
        im0, im1 = jnp.where(first, im, none), jnp.where(first, none, im)
        left = jnp.concatenate(
            [
                jnp.concatenate([re0, re1, im0, im1], axis=0),
                jnp.concatenate([-im0, -im1, re0, re1], axis=0),
            ],
            axis=1,
        )
        part, j = (0, i) if i < head else (1, i - head)
        bas = bas_refs[part][:, 2 * j : 2 * j + 2].reshape(2 * pair, comp).astype(BF)
        out_ref[:, 2 * i : 2 * i + 2] = dot(left, bas, NN).reshape(2, 2, cols, comp)
        copy(i).start()
    for i in range(pairs):
        copy(i).wait()


def prolong(here, there, basis, shape):
    vecs, comp = basis[0].shape[2:]
    cols = here.shape[1]
    pairs = shape[1] // 2
    return pl.pallas_call(
        prolong_kernel,
        in_specs=[whole()] * (2 + len(basis)),
        out_specs=pl.BlockSpec(memory_space=pltpu.HBM),
        out_shape=jax.ShapeDtypeStruct(shape, F32),
        scratch_shapes=[pltpu.VMEM(shape, F32), pltpu.SemaphoreType.DMA((pairs,))],
        compiler_params=pltpu.CompilerParams(vmem_limit_bytes=8 * MIB),
        cost_estimate=pl.CostEstimate(flops=64 * pairs * cols * vecs * comp, bytes_accessed=pairs * cols * comp * 16, transcendentals=0),
        name="prolong",
    )(here, there, *basis)


class Slice:
    def __init__(self, regions, shares):
        self.regions, self.shares = regions, shares

    def swap(self, value):
        return lax.ppermute(value, "eig", [(i, i ^ 1) for i in range(self.shares)])

    def cross(self, value, sender, region=0, chip=0):
        pairs = []
        for i in range(self.regions * self.shares):
            far = (i ^ (region * self.shares) ^ (2 * chip)) ^ 1
            pairs.append((i, far if i % 2 == sender else i ^ 1))
        return lax.ppermute(value, ("region", "eig"), pairs)

    def region_steps(self):
        step = 1
        while step < self.regions:
            four = 2 * step < self.regions
            yield [step, 2 * step, 3 * step] if four else [step]
            step *= 4 if four else 2

    def chip_steps(self):
        return range(1, self.shares // 2)


def total(terms):
    value = terms[0].astype(F32)
    for term in terms[1:]:
        value = value + term.astype(F32)
    return value


def add_kernel(scale_ref, *refs):
    *term_refs, out_ref = refs
    value = total([ref[...] for ref in term_refs])
    half = out_ref.shape[2] // 2
    if scale_ref is None:
        out_ref[...] = value.astype(BF)
    else:
        out_ref[:, :, :half] = value[:, :, :half].astype(BF)
        out_ref[:, :, half:] = (value[:, :, half:] * scale_ref[...]).astype(BF)


def add(terms, scale=None):
    kernel = functools.partial(add_kernel, None) if scale is None else add_kernel
    return pl.pallas_call(
        kernel,
        in_specs=([] if scale is None else [whole()]) + [whole()] * len(terms),
        out_specs=whole(),
        out_shape=jax.ShapeDtypeStruct(terms[0].shape, BF),
        compiler_params=pltpu.CompilerParams(vmem_limit_bytes=4 * MIB),
        cost_estimate=pl.CostEstimate(flops=terms[0].size * 2, bytes_accessed=terms[0].size * 4, transcendentals=0),
        name="add",
    )(*([] if scale is None else [scale]), *terms)


def shards(regions, shares, residual, basis, eigvecs, weights):
    place = Slice(regions, shares)
    core = (lax.axis_index("eig") % 2).astype(jnp.int32).reshape(1)
    blocks, vecs = basis.shape[1:3]
    count = eigvecs.shape[3]
    own = eigvecs.reshape(2, blocks * vecs, count)
    weights = weights.reshape(1, 1, count)

    part = project(residual, basis)
    chip_sum = add([part, place.swap(part)])
    sister = place.swap(lax.optimization_barrier((own, chip_sum[:1, :8, :128]))[0])
    holder = 1
    head = 2 * (blocks // 3)
    first = load(basis, 0, head, chip_sum)
    coarse = [chip_sum] + [place.cross(chip_sum, 0, chip=s) for s in place.chip_steps()]
    coarse, first = lax.optimization_barrier((coarse, first))

    start = holder
    active = (core == holder).astype(jnp.int32)
    value = contract(active, coarse, own, sister, weights.reshape(1, count))
    steps = list(place.region_steps())[::-1]
    for i, step in enumerate(steps):
        terms = [place.swap(value)] + [place.cross(value, holder, region=s) for s in step]
        holder = 1 - holder
        if i < len(steps) - 1:
            value = add(terms, weights if i == 0 else None)

    second = load(basis, head, blocks - head, value)
    terms, second = lax.optimization_barrier((terms, second))
    active = (core == holder).astype(jnp.int32)
    lifted = expand(active, terms, own, sister, holder == start)
    terms = [place.cross(lifted, holder, chip=s) for s in place.chip_steps()]
    here = jnp.where(core == holder, lifted, total(terms).astype(BF))
    return prolong(here, place.swap(here), (first, second), residual.shape)


def solution(mesh):
    split = P(None, "region", None, "eig")
    return jax.shard_map(
        functools.partial(shards, mesh.shape["region"], mesh.shape["eig"]),
        mesh=mesh,
        in_specs=(split, split, split, P("eig")),
        out_specs=split,
        check_vma=False,
    )
```

```python
import functools
import math

import jax
import jax.numpy as jnp
from jax import lax
from jax.experimental import pallas as pl
from jax.experimental.pallas import tpu as pltpu
from jax.sharding import PartitionSpec as P

BF = jnp.bfloat16
F32 = jnp.float32
NT = (((1,), (1,)), ((), ()))
NN = (((1,), (0,)), ((), ()))
MIB = 1 << 20


def dot(left, right, dims):
    return lax.dot_general(left, right, dims, preferred_element_type=F32)


def project_kernel(res_hbm, bas_hbm, sent_ref, res_ref, bas_ref, sem):
    cols, comp = res_ref.shape[2:]
    vecs = bas_ref.shape[2]
    pair = 2 * vecs
    pairs = sem.shape[1]

    def copies(i):
        two = pl.ds(2 * i, 2)
        return (
            pltpu.make_async_copy(res_hbm.at[:, two], res_ref.at[:, two], sem.at[0, i]),
            pltpu.make_async_copy(bas_hbm.at[:, two], bas_ref.at[:, two], sem.at[1, i]),
        )

    for i in range(pairs):
        for copy in copies(i):
            copy.start()
    first = lax.broadcasted_iota(jnp.int32, (cols, pair), 1) < vecs
    for i in range(pairs):
        for copy in copies(i):
            copy.wait()
        res = res_ref[:, 2 * i : 2 * i + 2].reshape(4 * cols, comp).astype(BF)
        bas = bas_ref[:, 2 * i : 2 * i + 2].reshape(2 * pair, comp).astype(BF)
        prod = dot(res, bas, NT)

        def part(row, lane):
            lanes = slice(lane * pair, (lane + 1) * pair)
            top = prod[2 * row * cols : (2 * row + 1) * cols, lanes]
            low = prod[(2 * row + 1) * cols : (2 * row + 2) * cols, lanes]
            return jnp.where(first, top, low)

        lanes = slice(i * pair, (i + 1) * pair)
        re, im = part(0, 0) + part(1, 1), part(1, 0) - part(0, 1)
        for row, value in ((0, re), (1, im)):
            sent_ref[row, :, lanes] = value.astype(BF)


def hbm(value):
    return pltpu.with_memory_space_constraint(value, pltpu.HBM)


def whole():
    return pl.BlockSpec(memory_space=pltpu.VMEM)


def scalar():
    return pl.BlockSpec(memory_space=pltpu.SMEM)


def project(residual, basis):
    _, blocks, cols, comp = residual.shape
    vecs = basis.shape[2]
    return pl.pallas_call(
        project_kernel,
        in_specs=[pl.BlockSpec(memory_space=pltpu.HBM)] * 2,
        out_specs=whole(),
        out_shape=jax.ShapeDtypeStruct((2, cols, blocks * vecs), BF),
        scratch_shapes=[
            pltpu.VMEM(residual.shape, F32),
            pltpu.VMEM(basis.shape, F32),
            pltpu.SemaphoreType.DMA((2, blocks // 2)),
        ],
        compiler_params=pltpu.CompilerParams(vmem_limit_bytes=18 * MIB),
        cost_estimate=pl.CostEstimate(
            flops=16 * blocks * cols * vecs * comp, bytes_accessed=(residual.size + basis.size) * 4, transcendentals=0
        ),
        name="project",
    )(hbm(residual), hbm(basis))


def contract_kernel(active, own_ref, sister_ref, wgt_ref, *refs):
    *coarse_refs, out_ref = refs
    cols, depth = coarse_refs[0].shape[1:]
    count = own_ref.shape[2]

    @pl.when(active[0] == 1)
    def _():
        coarse = total([ref[...] for ref in coarse_refs]).astype(BF).reshape(2 * cols, depth)
        for i, eig_ref in enumerate((own_ref, sister_ref)):
            by_re = dot(coarse, eig_ref[0], NN)
            by_im = dot(coarse, eig_ref[1], NN)
            re = by_re[:cols] + by_im[cols:]
            im = by_re[cols:] - by_im[:cols]
            if i == 0:
                re, im = re * wgt_ref[...], im * wgt_ref[...]
            out_ref[0, :, i * count : (i + 1) * count] = re.astype(BF)
            out_ref[1, :, i * count : (i + 1) * count] = im.astype(BF)


def contract(active, coarse, own, sister, weights):
    _, cols, depth = coarse[0].shape
    count = own.shape[2]
    return pl.pallas_call(
        contract_kernel,
        in_specs=[scalar()] + [whole()] * 3 + [whole()] * len(coarse),
        out_specs=whole(),
        out_shape=jax.ShapeDtypeStruct((2, cols, 2 * count), BF),
        compiler_params=pltpu.CompilerParams(vmem_limit_bytes=4 * MIB),
        cost_estimate=pl.CostEstimate(flops=16 * cols * depth * count, bytes_accessed=own.size * 4, transcendentals=0),
        name="contract",
    )(active, own, sister, weights, *coarse)


def turn_kernel(active, *refs):
    half = len(refs) // 2
    depth, count = refs[0].shape[1:]

    @pl.when(active[0] == 1)
    def _():
        for from_ref, to_ref in zip(refs[:half], refs[half:]):
            for part in range(from_ref.shape[0]):
                for row in range(0, depth, count):
                    to_ref[part, :, row : row + count] = from_ref[part, row : row + count, :].T


def turn(active, arrays, after):
    arrays = lax.optimization_barrier((arrays, after))[0]
    shapes = [(a.shape[0], a.shape[2], a.shape[1]) for a in arrays]
    return pl.pallas_call(
        turn_kernel,
        in_specs=[scalar()] + [whole()] * len(arrays),
        out_specs=[whole()] * len(arrays),
        out_shape=[pltpu.VMEM(shape, a.dtype) for shape, a in zip(shapes, arrays)],
        compiler_params=pltpu.CompilerParams(vmem_limit_bytes=4 * MIB),
        cost_estimate=pl.CostEstimate(flops=0, bytes_accessed=sum(a.size for a in arrays) * 4, transcendentals=0),
        name="turn",
    )(active, *arrays)


def expand_kernel(own_first, active, own_ref, sister_ref, *refs):
    *wgt_refs, out_ref = refs
    cols = out_ref.shape[1]
    count = own_ref.shape[1]

    @pl.when(active[0] == 1)
    def _():
        whole_wgt = total([ref[...] for ref in wgt_refs]).astype(BF)
        re = im = None
        for i, eig_ref in enumerate((own_ref, sister_ref) if own_first else (sister_ref, own_ref)):
            weighted = whole_wgt[:, :, i * count : (i + 1) * count].reshape(2 * cols, count)
            by_re = dot(weighted, eig_ref[0], NN)
            by_im = dot(weighted, eig_ref[1], NN)
            re = by_re[:cols] - by_im[cols:] + (0 if re is None else re)
            im = by_re[cols:] + by_im[:cols] + (0 if im is None else im)
        out_ref[0] = re.astype(BF)
        out_ref[1] = im.astype(BF)


def expand(active, weighted, own, sister, own_first):
    cols = weighted[0].shape[1]
    count, depth = own.shape[1:]
    return pl.pallas_call(
        functools.partial(expand_kernel, own_first),
        in_specs=[scalar()] + [whole()] * 2 + [whole()] * len(weighted),
        out_specs=whole(),
        out_shape=jax.ShapeDtypeStruct((2, cols, depth), BF),
        compiler_params=pltpu.CompilerParams(vmem_limit_bytes=4 * MIB),
        cost_estimate=pl.CostEstimate(flops=16 * cols * depth * count, bytes_accessed=own.size * 4, transcendentals=0),
        name="expand",
    )(active, own, sister, *weighted)


def load_kernel(start, from_hbm, to_ref, sem):
    copy = pltpu.make_async_copy(from_hbm.at[:, pl.ds(start, to_ref.shape[1])], to_ref, sem)
    copy.start()
    copy.wait()


def load(value, start, size, after):
    shape = value.shape[:1] + (size,) + value.shape[2:]
    return pl.pallas_call(
        functools.partial(load_kernel, start),
        in_specs=[pl.BlockSpec(memory_space=pltpu.HBM)],
        out_specs=whole(),
        out_shape=pltpu.VMEM(shape, value.dtype),
        scratch_shapes=[pltpu.SemaphoreType.DMA],
        compiler_params=pltpu.CompilerParams(vmem_limit_bytes=4 * MIB),
        cost_estimate=pl.CostEstimate(flops=0, bytes_accessed=math.prod(shape) * 4, transcendentals=0),
        name="load",
    )(hbm(lax.optimization_barrier((value, after))[0]))


def prolong_kernel(here_ref, there_ref, *refs):
    *bas_refs, out_hbm, out_ref, sem = refs
    cols, comp = out_ref.shape[2:]
    pair = 2 * bas_refs[0].shape[2]
    pairs = sem.shape[0]
    head = bas_refs[0].shape[1] // 2
    first = lax.broadcasted_iota(jnp.int32, (cols, pair), 1) < pair // 2

    def copy(i):
        two = pl.ds(2 * i, 2)
        return pltpu.make_async_copy(out_ref.at[:, two], out_hbm.at[:, two], sem.at[i])

    for i in range(pairs):
        lanes = slice(i * pair, (i + 1) * pair)
        re, im = (total([ref[row, :, lanes] for ref in (here_ref, there_ref)]).astype(BF) for row in range(2))
        none = jnp.zeros_like(re)
        re0, re1 = jnp.where(first, re, none), jnp.where(first, none, re)
        im0, im1 = jnp.where(first, im, none), jnp.where(first, none, im)
        left = jnp.concatenate(
            [
                jnp.concatenate([re0, re1, im0, im1], axis=0),
                jnp.concatenate([-im0, -im1, re0, re1], axis=0),
            ],
            axis=1,
        )
        part, j = (0, i) if i < head else (1, i - head)
        bas = bas_refs[part][:, 2 * j : 2 * j + 2].reshape(2 * pair, comp).astype(BF)
        out_ref[:, 2 * i : 2 * i + 2] = dot(left, bas, NN).reshape(2, 2, cols, comp)
        copy(i).start()
    for i in range(pairs):
        copy(i).wait()


def prolong(here, there, basis, shape):
    vecs, comp = basis[0].shape[2:]
    cols = here.shape[1]
    pairs = shape[1] // 2
    return pl.pallas_call(
        prolong_kernel,
        in_specs=[whole()] * (2 + len(basis)),
        out_specs=pl.BlockSpec(memory_space=pltpu.HBM),
        out_shape=jax.ShapeDtypeStruct(shape, F32),
        scratch_shapes=[pltpu.VMEM(shape, F32), pltpu.SemaphoreType.DMA((pairs,))],
        compiler_params=pltpu.CompilerParams(vmem_limit_bytes=8 * MIB),
        cost_estimate=pl.CostEstimate(flops=64 * pairs * cols * vecs * comp, bytes_accessed=pairs * cols * comp * 16, transcendentals=0),
        name="prolong",
    )(here, there, *basis)


class Slice:
    def __init__(self, regions, shares):
        self.regions, self.shares = regions, shares

    def swap(self, value):
        return lax.ppermute(value, "eig", [(i, i ^ 1) for i in range(self.shares)])

    def cross(self, value, sender, region=0, chip=0):
        pairs = []
        for i in range(self.regions * self.shares):
            far = (i ^ (region * self.shares) ^ (2 * chip)) ^ 1
            pairs.append((i, far if i % 2 == sender else i ^ 1))
        return lax.ppermute(value, ("region", "eig"), pairs)

    def region_steps(self):
        step = 1
        while step < self.regions:
            four = 2 * step < self.regions
            yield [step, 2 * step, 3 * step] if four else [step]
            step *= 4 if four else 2

    def chip_steps(self):
        return range(1, self.shares // 2)


def total(terms):
    value = terms[0].astype(F32)
    for term in terms[1:]:
        value = value + term.astype(F32)
    return value


def add_kernel(scale_ref, *refs):
    *term_refs, out_ref = refs
    value = total([ref[...] for ref in term_refs])
    half = out_ref.shape[2] // 2
    if scale_ref is None:
        out_ref[...] = value.astype(BF)
    else:
        out_ref[:, :, :half] = value[:, :, :half].astype(BF)
        out_ref[:, :, half:] = (value[:, :, half:] * scale_ref[...]).astype(BF)


def add(terms, scale=None):
    kernel = functools.partial(add_kernel, None) if scale is None else add_kernel
    return pl.pallas_call(
        kernel,
        in_specs=([] if scale is None else [whole()]) + [whole()] * len(terms),
        out_specs=whole(),
        out_shape=jax.ShapeDtypeStruct(terms[0].shape, BF),
        compiler_params=pltpu.CompilerParams(vmem_limit_bytes=4 * MIB),
        cost_estimate=pl.CostEstimate(flops=terms[0].size * 2, bytes_accessed=terms[0].size * 4, transcendentals=0),
        name="add",
    )(*([] if scale is None else [scale]), *terms)


def shards(regions, shares, residual, basis, eigvecs, weights):
    place = Slice(regions, shares)
    core = (lax.axis_index("eig") % 2).astype(jnp.int32).reshape(1)
    blocks, vecs = basis.shape[1:3]
    count = eigvecs.shape[3]
    own = eigvecs.reshape(2, blocks * vecs, count)
    weights = weights.reshape(1, 1, count)

    part = project(residual, basis)
    chip_sum = add([part, place.swap(part)])
    sister = place.swap(lax.optimization_barrier((own, chip_sum[:1, :8, :128]))[0])
    holder = 1
    head = 2 * (blocks // 3)
    first = load(basis, 0, head, chip_sum)
    coarse = [chip_sum] + [place.cross(chip_sum, 0, chip=s) for s in place.chip_steps()]
    coarse, first = lax.optimization_barrier((coarse, first))

    start = holder
    active = (core == holder).astype(jnp.int32)
    value = contract(active, coarse, own, sister, weights.reshape(1, count))
    steps = list(place.region_steps())[::-1]
    for i, step in enumerate(steps):
        terms = [place.swap(value)] + [place.cross(value, holder, region=s) for s in step]
        holder = 1 - holder
        if i == 0:
            last = (start + len(steps)) % 2
            active = (core == last).astype(jnp.int32)
            turned = turn(active, [own, sister], value)
            terms, turned = lax.optimization_barrier((terms, turned))
        if i < len(steps) - 1:
            value = add(terms, weights if i == 0 else None)

    second = load(basis, head, blocks - head, value)
    terms, second = lax.optimization_barrier((terms, second))
    lifted = expand(active, terms, *turned, holder == start)
    terms = [place.cross(lifted, holder, chip=s) for s in place.chip_steps()]
    here = jnp.where(core == holder, lifted, total(terms).astype(BF))
    return prolong(here, place.swap(here), (first, second), residual.shape)


def solution(mesh):
    split = P(None, "region", None, "eig")
    return jax.shard_map(
        functools.partial(shards, mesh.shape["region"], mesh.shape["eig"]),
        mesh=mesh,
        in_specs=(split, split, split, P("eig")),
        out_specs=split,
        check_vma=False,
    )
```

```python
import functools
import math

import jax
import jax.numpy as jnp
from jax import lax
from jax.experimental import pallas as pl
from jax.experimental.pallas import tpu as pltpu
from jax.sharding import PartitionSpec as P

BF = jnp.bfloat16
F32 = jnp.float32
NT = (((1,), (1,)), ((), ()))
NN = (((1,), (0,)), ((), ()))
MIB = 1 << 20


def dot(left, right, dims):
    return lax.dot_general(left, right, dims, preferred_element_type=F32)


def project_kernel(res_hbm, bas_hbm, sent_ref, res_ref, bas_ref, sem):
    cols, comp = res_ref.shape[2:]
    vecs = bas_ref.shape[2]
    pair = 2 * vecs
    pairs = sem.shape[1]

    def copies(i):
        two = pl.ds(2 * i, 2)
        return (
            pltpu.make_async_copy(res_hbm.at[:, two], res_ref.at[:, two], sem.at[0, i]),
            pltpu.make_async_copy(bas_hbm.at[:, two], bas_ref.at[:, two], sem.at[1, i]),
        )

    for i in range(pairs):
        for copy in copies(i):
            copy.start()
    first = lax.broadcasted_iota(jnp.int32, (cols, pair), 1) < vecs
    for i in range(pairs):
        for copy in copies(i):
            copy.wait()
        res = res_ref[:, 2 * i : 2 * i + 2].reshape(4 * cols, comp).astype(BF)
        bas = bas_ref[:, 2 * i : 2 * i + 2].reshape(2 * pair, comp).astype(BF)
        prod = dot(res, bas, NT)

        def part(row, lane):
            lanes = slice(lane * pair, (lane + 1) * pair)
            top = prod[2 * row * cols : (2 * row + 1) * cols, lanes]
            low = prod[(2 * row + 1) * cols : (2 * row + 2) * cols, lanes]
            return jnp.where(first, top, low)

        lanes = slice(i * pair, (i + 1) * pair)
        re, im = part(0, 0) + part(1, 1), part(1, 0) - part(0, 1)
        for row, value in ((0, re), (1, im)):
            sent_ref[row, :, lanes] = value.astype(BF)


def hbm(value):
    return pltpu.with_memory_space_constraint(value, pltpu.HBM)


def whole():
    return pl.BlockSpec(memory_space=pltpu.VMEM)


def scalar():
    return pl.BlockSpec(memory_space=pltpu.SMEM)


def project(residual, basis):
    _, blocks, cols, comp = residual.shape
    vecs = basis.shape[2]
    return pl.pallas_call(
        project_kernel,
        in_specs=[pl.BlockSpec(memory_space=pltpu.HBM)] * 2,
        out_specs=whole(),
        out_shape=jax.ShapeDtypeStruct((2, cols, blocks * vecs), BF),
        scratch_shapes=[
            pltpu.VMEM(residual.shape, F32),
            pltpu.VMEM(basis.shape, F32),
            pltpu.SemaphoreType.DMA((2, blocks // 2)),
        ],
        compiler_params=pltpu.CompilerParams(vmem_limit_bytes=18 * MIB),
        cost_estimate=pl.CostEstimate(
            flops=16 * blocks * cols * vecs * comp, bytes_accessed=(residual.size + basis.size) * 4, transcendentals=0
        ),
        name="project",
    )(hbm(residual), hbm(basis))


def contract_kernel(active, own_ref, sister_ref, wgt_ref, *refs):
    *coarse_refs, out_ref = refs
    cols, depth = coarse_refs[0].shape[1:]
    count = own_ref.shape[2]

    @pl.when(active[0] == 1)
    def _():
        coarse = total([ref[...] for ref in coarse_refs]).astype(BF).reshape(2 * cols, depth)
        for i, eig_ref in enumerate((own_ref, sister_ref)):
            by_re = dot(coarse, eig_ref[0], NN)
            by_im = dot(coarse, eig_ref[1], NN)
            re = by_re[:cols] + by_im[cols:]
            im = by_re[cols:] - by_im[:cols]
            if i == 0:
                re, im = re * wgt_ref[...], im * wgt_ref[...]
            out_ref[0, :, i * count : (i + 1) * count] = re.astype(BF)
            out_ref[1, :, i * count : (i + 1) * count] = im.astype(BF)


def contract(active, coarse, own, sister, weights):
    _, cols, depth = coarse[0].shape
    count = own.shape[2]
    return pl.pallas_call(
        contract_kernel,
        in_specs=[scalar()] + [whole()] * 3 + [whole()] * len(coarse),
        out_specs=whole(),
        out_shape=jax.ShapeDtypeStruct((2, cols, 2 * count), BF),
        compiler_params=pltpu.CompilerParams(vmem_limit_bytes=4 * MIB),
        cost_estimate=pl.CostEstimate(flops=16 * cols * depth * count, bytes_accessed=own.size * 4, transcendentals=0),
        name="contract",
    )(active, own, sister, weights, *coarse)


def turn_kernel(active, *refs):
    half = len(refs) // 2
    depth, count = refs[0].shape[1:]

    @pl.when(active[0] == 1)
    def _():
        for from_ref, to_ref in zip(refs[:half], refs[half:]):
            for part in range(from_ref.shape[0]):
                for row in range(0, depth, count):
                    to_ref[part, :, row : row + count] = from_ref[part, row : row + count, :].T


def turn(active, arrays, after):
    arrays = lax.optimization_barrier((arrays, after))[0]
    shapes = [(a.shape[0], a.shape[2], a.shape[1]) for a in arrays]
    return pl.pallas_call(
        turn_kernel,
        in_specs=[scalar()] + [whole()] * len(arrays),
        out_specs=[whole()] * len(arrays),
        out_shape=[pltpu.VMEM(shape, a.dtype) for shape, a in zip(shapes, arrays)],
        compiler_params=pltpu.CompilerParams(vmem_limit_bytes=4 * MIB),
        cost_estimate=pl.CostEstimate(flops=0, bytes_accessed=sum(a.size for a in arrays) * 4, transcendentals=0),
        name="turn",
    )(active, *arrays)


def expand_kernel(own_first, active, own_ref, sister_ref, *refs):
    *wgt_refs, out_ref = refs
    cols = out_ref.shape[1]
    count = own_ref.shape[1]

    @pl.when(active[0] == 1)
    def _():
        whole_wgt = total([ref[...] for ref in wgt_refs]).astype(BF)
        re = im = None
        for i, eig_ref in enumerate((own_ref, sister_ref) if own_first else (sister_ref, own_ref)):
            weighted = whole_wgt[:, :, i * count : (i + 1) * count].reshape(2 * cols, count)
            by_re = dot(weighted, eig_ref[0], NN)
            by_im = dot(weighted, eig_ref[1], NN)
            re = by_re[:cols] - by_im[cols:] + (0 if re is None else re)
            im = by_re[cols:] + by_im[:cols] + (0 if im is None else im)
        out_ref[0] = re.astype(BF)
        out_ref[1] = im.astype(BF)


def expand(active, weighted, own, sister, own_first):
    cols = weighted[0].shape[1]
    count, depth = own.shape[1:]
    return pl.pallas_call(
        functools.partial(expand_kernel, own_first),
        in_specs=[scalar()] + [whole()] * 2 + [whole()] * len(weighted),
        out_specs=whole(),
        out_shape=jax.ShapeDtypeStruct((2, cols, depth), BF),
        compiler_params=pltpu.CompilerParams(vmem_limit_bytes=4 * MIB),
        cost_estimate=pl.CostEstimate(flops=16 * cols * depth * count, bytes_accessed=own.size * 4, transcendentals=0),
        name="expand",
    )(active, own, sister, *weighted)


def load_kernel(start, from_hbm, to_ref, sem):
    copy = pltpu.make_async_copy(from_hbm.at[:, pl.ds(start, to_ref.shape[1])], to_ref, sem)
    copy.start()
    copy.wait()


def load(value, start, size, after):
    shape = value.shape[:1] + (size,) + value.shape[2:]
    return pl.pallas_call(
        functools.partial(load_kernel, start),
        in_specs=[pl.BlockSpec(memory_space=pltpu.HBM)],
        out_specs=whole(),
        out_shape=pltpu.VMEM(shape, value.dtype),
        scratch_shapes=[pltpu.SemaphoreType.DMA],
        compiler_params=pltpu.CompilerParams(vmem_limit_bytes=4 * MIB),
        cost_estimate=pl.CostEstimate(flops=0, bytes_accessed=math.prod(shape) * 4, transcendentals=0),
        name="load",
    )(hbm(lax.optimization_barrier((value, after))[0]))


def prolong_kernel(here_ref, there_ref, *refs):
    *bas_refs, out_hbm, out_ref, sem = refs
    cols, comp = out_ref.shape[2:]
    pair = 2 * bas_refs[0].shape[2]
    pairs = sem.shape[0]
    head = bas_refs[0].shape[1] // 2
    first = lax.broadcasted_iota(jnp.int32, (cols, pair), 1) < pair // 2

    def copy(i):
        two = pl.ds(2 * i, 2)
        return pltpu.make_async_copy(out_ref.at[:, two], out_hbm.at[:, two], sem.at[i])

    for i in range(pairs):
        lanes = slice(i * pair, (i + 1) * pair)
        re, im = (total([ref[row, :, lanes] for ref in (here_ref, there_ref)]).astype(BF) for row in range(2))
        none = jnp.zeros_like(re)
        re0, re1 = jnp.where(first, re, none), jnp.where(first, none, re)
        im0, im1 = jnp.where(first, im, none), jnp.where(first, none, im)
        left = jnp.concatenate(
            [
                jnp.concatenate([re0, re1, im0, im1], axis=0),
                jnp.concatenate([-im0, -im1, re0, re1], axis=0),
            ],
            axis=1,
        )
        part, j = (0, i) if i < head else (1, i - head)
        bas = bas_refs[part][:, 2 * j : 2 * j + 2].reshape(2 * pair, comp).astype(BF)
        out_ref[:, 2 * i : 2 * i + 2] = dot(left, bas, NN).reshape(2, 2, cols, comp)
        copy(i).start()
    for i in range(pairs):
        copy(i).wait()


def prolong(here, there, basis, shape):
    vecs, comp = basis[0].shape[2:]
    cols = here.shape[1]
    pairs = shape[1] // 2
    return pl.pallas_call(
        prolong_kernel,
        in_specs=[whole()] * (2 + len(basis)),
        out_specs=pl.BlockSpec(memory_space=pltpu.HBM),
        out_shape=jax.ShapeDtypeStruct(shape, F32),
        scratch_shapes=[pltpu.VMEM(shape, F32), pltpu.SemaphoreType.DMA((pairs,))],
        compiler_params=pltpu.CompilerParams(vmem_limit_bytes=8 * MIB),
        cost_estimate=pl.CostEstimate(flops=64 * pairs * cols * vecs * comp, bytes_accessed=pairs * cols * comp * 16, transcendentals=0),
        name="prolong",
    )(here, there, *basis)


class Slice:
    def __init__(self, regions, shares):
        self.regions, self.shares = regions, shares

    def swap(self, value):
        return lax.ppermute(value, "eig", [(i, i ^ 1) for i in range(self.shares)])

    def cross(self, value, sender, region=0, chip=0):
        pairs = []
        for i in range(self.regions * self.shares):
            far = (i ^ (region * self.shares) ^ (2 * chip)) ^ 1
            pairs.append((i, far if i % 2 == sender else i ^ 1))
        return lax.ppermute(value, ("region", "eig"), pairs)

    def region_steps(self):
        step = 1
        while step < self.regions:
            four = 2 * step < self.regions
            yield [2 * step, step, 3 * step] if four else [step]
            step *= 4 if four else 2

    def chip_steps(self):
        return range(1, self.shares // 2)


def total(terms):
    value = terms[0].astype(F32)
    for term in terms[1:]:
        value = value + term.astype(F32)
    return value


def add_kernel(scale_ref, *refs):
    *term_refs, out_ref = refs
    value = total([ref[...] for ref in term_refs])
    half = out_ref.shape[2] // 2
    if scale_ref is None:
        out_ref[...] = value.astype(BF)
    else:
        out_ref[:, :, :half] = value[:, :, :half].astype(BF)
        out_ref[:, :, half:] = (value[:, :, half:] * scale_ref[...]).astype(BF)


def add(terms, scale=None):
    kernel = functools.partial(add_kernel, None) if scale is None else add_kernel
    return pl.pallas_call(
        kernel,
        in_specs=([] if scale is None else [whole()]) + [whole()] * len(terms),
        out_specs=whole(),
        out_shape=jax.ShapeDtypeStruct(terms[0].shape, BF),
        compiler_params=pltpu.CompilerParams(vmem_limit_bytes=4 * MIB),
        cost_estimate=pl.CostEstimate(flops=terms[0].size * 2, bytes_accessed=terms[0].size * 4, transcendentals=0),
        name="add",
    )(*([] if scale is None else [scale]), *terms)


def shards(regions, shares, residual, basis, eigvecs, weights):
    place = Slice(regions, shares)
    core = (lax.axis_index("eig") % 2).astype(jnp.int32).reshape(1)
    blocks, vecs = basis.shape[1:3]
    count = eigvecs.shape[3]
    own = eigvecs.reshape(2, blocks * vecs, count)
    weights = weights.reshape(1, 1, count)

    part = project(residual, basis)
    chip_sum = add([part, place.swap(part)])
    sister = place.swap(lax.optimization_barrier((own, chip_sum[:1, :8, :128]))[0])
    holder = 0
    head = 2 * (blocks // 3)
    first = load(basis, 0, head, chip_sum)
    coarse = [chip_sum] + [place.cross(chip_sum, 1 - holder, chip=s) for s in place.chip_steps()]
    coarse, first = lax.optimization_barrier((coarse, first))

    start = holder
    active = (core == holder).astype(jnp.int32)
    value = contract(active, coarse, own, sister, weights.reshape(1, count))
    steps = list(place.region_steps())[::-1]
    for i, step in enumerate(steps):
        terms = [place.swap(value)] + [place.cross(value, holder, region=s) for s in step]
        holder = 1 - holder
        if i == 0:
            last = (start + len(steps)) % 2
            active = (core == last).astype(jnp.int32)
            turned = turn(active, [own, sister], value)
            terms, turned = lax.optimization_barrier((terms, turned))
        if i < len(steps) - 1:
            value = add(terms, weights if i == 0 else None)

    second = load(basis, head, blocks - head, value)
    terms, second = lax.optimization_barrier((terms, second))
    lifted = expand(active, terms, *turned, holder == start)
    terms = [place.cross(lifted, holder, chip=s) for s in place.chip_steps()]
    here = jnp.where(core == holder, lifted, total(terms).astype(BF))
    return prolong(here, place.swap(here), (first, second), residual.shape)


def solution(mesh):
    split = P(None, "region", None, "eig")
    return jax.shard_map(
        functools.partial(shards, mesh.shape["region"], mesh.shape["eig"]),
        mesh=mesh,
        in_specs=(split, split, split, P("eig")),
        out_specs=split,
        check_vma=False,
    )
```

```python
import functools
import math

import jax
import jax.numpy as jnp
from jax import lax
from jax.experimental import pallas as pl
from jax.experimental.pallas import tpu as pltpu
from jax.sharding import PartitionSpec as P

BF = jnp.bfloat16
F32 = jnp.float32
NT = (((1,), (1,)), ((), ()))
NN = (((1,), (0,)), ((), ()))
MIB = 1 << 20


def dot(left, right, dims):
    return lax.dot_general(left, right, dims, preferred_element_type=F32)


def project_kernel(res_hbm, bas_hbm, sent_ref, res_ref, bas_ref, sem):
    cols, comp = res_ref.shape[2:]
    vecs = bas_ref.shape[2]
    pair = 2 * vecs
    pairs = sem.shape[1]

    def copies(i):
        two = pl.ds(2 * i, 2)
        return (
            pltpu.make_async_copy(res_hbm.at[:, two], res_ref.at[:, two], sem.at[0, i]),
            pltpu.make_async_copy(bas_hbm.at[:, two], bas_ref.at[:, two], sem.at[1, i]),
        )

    for i in range(pairs):
        for copy in copies(i):
            copy.start()
    first = lax.broadcasted_iota(jnp.int32, (cols, pair), 1) < vecs
    for i in range(pairs):
        for copy in copies(i):
            copy.wait()
        res = res_ref[:, 2 * i : 2 * i + 2].reshape(4 * cols, comp).astype(BF)
        bas = bas_ref[:, 2 * i : 2 * i + 2].reshape(2 * pair, comp).astype(BF)
        prod = dot(res, bas, NT)

        def part(row, lane):
            lanes = slice(lane * pair, (lane + 1) * pair)
            top = prod[2 * row * cols : (2 * row + 1) * cols, lanes]
            low = prod[(2 * row + 1) * cols : (2 * row + 2) * cols, lanes]
            return jnp.where(first, top, low)

        lanes = slice(i * pair, (i + 1) * pair)
        re, im = part(0, 0) + part(1, 1), part(1, 0) - part(0, 1)
        for row, value in ((0, re), (1, im)):
            sent_ref[row, :, lanes] = value.astype(BF)


def hbm(value):
    return pltpu.with_memory_space_constraint(value, pltpu.HBM)


def whole():
    return pl.BlockSpec(memory_space=pltpu.VMEM)


def scalar():
    return pl.BlockSpec(memory_space=pltpu.SMEM)


def project(residual, basis):
    _, blocks, cols, comp = residual.shape
    vecs = basis.shape[2]
    return pl.pallas_call(
        project_kernel,
        in_specs=[pl.BlockSpec(memory_space=pltpu.HBM)] * 2,
        out_specs=whole(),
        out_shape=jax.ShapeDtypeStruct((2, cols, blocks * vecs), BF),
        scratch_shapes=[
            pltpu.VMEM(residual.shape, F32),
            pltpu.VMEM(basis.shape, F32),
            pltpu.SemaphoreType.DMA((2, blocks // 2)),
        ],
        compiler_params=pltpu.CompilerParams(vmem_limit_bytes=18 * MIB),
        cost_estimate=pl.CostEstimate(
            flops=16 * blocks * cols * vecs * comp, bytes_accessed=(residual.size + basis.size) * 4, transcendentals=0
        ),
        name="project",
    )(hbm(residual), hbm(basis))


def contract_kernel(active, own_ref, sister_ref, wgt_ref, *refs):
    *coarse_refs, out_ref = refs
    cols, depth = coarse_refs[0].shape[1:]
    count = own_ref.shape[2]

    @pl.when(active[0] == 1)
    def _():
        coarse = total([ref[...] for ref in coarse_refs]).astype(BF).reshape(2 * cols, depth)
        for i, eig_ref in enumerate((own_ref, sister_ref)):
            by_re = dot(coarse, eig_ref[0], NN)
            by_im = dot(coarse, eig_ref[1], NN)
            re = by_re[:cols] + by_im[cols:]
            im = by_re[cols:] - by_im[:cols]
            if i == 0:
                re, im = re * wgt_ref[...], im * wgt_ref[...]
            out_ref[0, :, i * count : (i + 1) * count] = re.astype(BF)
            out_ref[1, :, i * count : (i + 1) * count] = im.astype(BF)


def contract(active, coarse, own, sister, weights):
    _, cols, depth = coarse[0].shape
    count = own.shape[2]
    return pl.pallas_call(
        contract_kernel,
        in_specs=[scalar()] + [whole()] * 3 + [whole()] * len(coarse),
        out_specs=whole(),
        out_shape=jax.ShapeDtypeStruct((2, cols, 2 * count), BF),
        compiler_params=pltpu.CompilerParams(vmem_limit_bytes=4 * MIB),
        cost_estimate=pl.CostEstimate(flops=16 * cols * depth * count, bytes_accessed=own.size * 4, transcendentals=0),
        name="contract",
    )(active, own, sister, weights, *coarse)


def turn_kernel(active, *refs):
    half = len(refs) // 2
    depth, count = refs[0].shape[1:]

    @pl.when(active[0] == 1)
    def _():
        for from_ref, to_ref in zip(refs[:half], refs[half:]):
            for part in range(from_ref.shape[0]):
                for row in range(0, depth, count):
                    to_ref[part, :, row : row + count] = from_ref[part, row : row + count, :].T


def turn(active, arrays, after):
    arrays = lax.optimization_barrier((arrays, after))[0]
    shapes = [(a.shape[0], a.shape[2], a.shape[1]) for a in arrays]
    return pl.pallas_call(
        turn_kernel,
        in_specs=[scalar()] + [whole()] * len(arrays),
        out_specs=[whole()] * len(arrays),
        out_shape=[pltpu.VMEM(shape, a.dtype) for shape, a in zip(shapes, arrays)],
        compiler_params=pltpu.CompilerParams(vmem_limit_bytes=4 * MIB),
        cost_estimate=pl.CostEstimate(flops=0, bytes_accessed=sum(a.size for a in arrays) * 4, transcendentals=0),
        name="turn",
    )(active, *arrays)


def expand_kernel(own_first, active, own_ref, sister_ref, *refs):
    *wgt_refs, out_ref = refs
    cols = out_ref.shape[1]
    count = own_ref.shape[1]

    @pl.when(active[0] == 1)
    def _():
        whole_wgt = total([ref[...] for ref in wgt_refs]).astype(BF)
        re = im = None
        for i, eig_ref in enumerate((own_ref, sister_ref) if own_first else (sister_ref, own_ref)):
            weighted = whole_wgt[:, :, i * count : (i + 1) * count].reshape(2 * cols, count)
            by_re = dot(weighted, eig_ref[0], NN)
            by_im = dot(weighted, eig_ref[1], NN)
            re = by_re[:cols] - by_im[cols:] + (0 if re is None else re)
            im = by_re[cols:] + by_im[:cols] + (0 if im is None else im)
        out_ref[0] = re.astype(BF)
        out_ref[1] = im.astype(BF)


def expand(active, weighted, own, sister, own_first):
    cols = weighted[0].shape[1]
    count, depth = own.shape[1:]
    return pl.pallas_call(
        functools.partial(expand_kernel, own_first),
        in_specs=[scalar()] + [whole()] * 2 + [whole()] * len(weighted),
        out_specs=whole(),
        out_shape=jax.ShapeDtypeStruct((2, cols, depth), BF),
        compiler_params=pltpu.CompilerParams(vmem_limit_bytes=4 * MIB),
        cost_estimate=pl.CostEstimate(flops=16 * cols * depth * count, bytes_accessed=own.size * 4, transcendentals=0),
        name="expand",
    )(active, own, sister, *weighted)


def load_kernel(start, from_hbm, to_ref, sem):
    copy = pltpu.make_async_copy(from_hbm.at[:, pl.ds(start, to_ref.shape[1])], to_ref, sem)
    copy.start()
    copy.wait()


def load(value, start, size, after):
    shape = value.shape[:1] + (size,) + value.shape[2:]
    return pl.pallas_call(
        functools.partial(load_kernel, start),
        in_specs=[pl.BlockSpec(memory_space=pltpu.HBM)],
        out_specs=whole(),
        out_shape=pltpu.VMEM(shape, value.dtype),
        scratch_shapes=[pltpu.SemaphoreType.DMA],
        compiler_params=pltpu.CompilerParams(vmem_limit_bytes=4 * MIB),
        cost_estimate=pl.CostEstimate(flops=0, bytes_accessed=math.prod(shape) * 4, transcendentals=0),
        name="load",
    )(hbm(lax.optimization_barrier((value, after))[0]))


def prolong_kernel(here_ref, there_ref, *refs):
    *bas_refs, out_hbm, out_ref, sem = refs
    cols, comp = out_ref.shape[2:]
    pair = 2 * bas_refs[0].shape[2]
    pairs = sem.shape[0]
    head = bas_refs[0].shape[1] // 2
    first = lax.broadcasted_iota(jnp.int32, (cols, pair), 1) < pair // 2

    def copy(i):
        two = pl.ds(2 * i, 2)
        return pltpu.make_async_copy(out_ref.at[:, two], out_hbm.at[:, two], sem.at[i])

    for i in range(pairs):
        lanes = slice(i * pair, (i + 1) * pair)
        re, im = (total([ref[row, :, lanes] for ref in (here_ref, there_ref)]).astype(BF) for row in range(2))
        none = jnp.zeros_like(re)
        re0, re1 = jnp.where(first, re, none), jnp.where(first, none, re)
        im0, im1 = jnp.where(first, im, none), jnp.where(first, none, im)
        left = jnp.concatenate(
            [
                jnp.concatenate([re0, re1, im0, im1], axis=0),
                jnp.concatenate([-im0, -im1, re0, re1], axis=0),
            ],
            axis=1,
        )
        part, j = (0, i) if i < head else (1, i - head)
        bas = bas_refs[part][:, 2 * j : 2 * j + 2].reshape(2 * pair, comp).astype(BF)
        out_ref[:, 2 * i : 2 * i + 2] = dot(left, bas, NN).reshape(2, 2, cols, comp)
        copy(i).start()
    for i in range(pairs):
        copy(i).wait()


def prolong(here, there, basis, shape):
    vecs, comp = basis[0].shape[2:]
    cols = here.shape[1]
    pairs = shape[1] // 2
    return pl.pallas_call(
        prolong_kernel,
        in_specs=[whole()] * (2 + len(basis)),
        out_specs=pl.BlockSpec(memory_space=pltpu.HBM),
        out_shape=jax.ShapeDtypeStruct(shape, F32),
        scratch_shapes=[pltpu.VMEM(shape, F32), pltpu.SemaphoreType.DMA((pairs,))],
        compiler_params=pltpu.CompilerParams(vmem_limit_bytes=8 * MIB),
        cost_estimate=pl.CostEstimate(flops=64 * pairs * cols * vecs * comp, bytes_accessed=pairs * cols * comp * 16, transcendentals=0),
        name="prolong",
    )(here, there, *basis)


class Slice:
    def __init__(self, regions, shares):
        self.regions, self.shares = regions, shares

    def swap(self, value):
        return lax.ppermute(value, "eig", [(i, i ^ 1) for i in range(self.shares)])

    def cross(self, value, sender, region=0, chip=0):
        pairs = []
        for i in range(self.regions * self.shares):
            far = (i ^ (region * self.shares) ^ (2 * chip)) ^ 1
            pairs.append((i, far if i % 2 == sender else i ^ 1))
        return lax.ppermute(value, ("region", "eig"), pairs)

    def region_steps(self):
        step = 1
        while step < self.regions:
            four = 2 * step < self.regions
            yield [2 * step, step, 3 * step] if four else [step]
            step *= 4 if four else 2

    def chip_steps(self):
        return range(1, self.shares // 2)


def total(terms):
    value = terms[0].astype(F32)
    for term in terms[1:]:
        value = value + term.astype(F32)
    return value


def add_kernel(scale_ref, *refs):
    *term_refs, out_ref = refs
    value = total([ref[...] for ref in term_refs])
    half = out_ref.shape[2] // 2
    if scale_ref is None:
        out_ref[...] = value.astype(BF)
    else:
        out_ref[:, :, :half] = value[:, :, :half].astype(BF)
        out_ref[:, :, half:] = (value[:, :, half:] * scale_ref[...]).astype(BF)


def add(terms, scale=None):
    kernel = functools.partial(add_kernel, None) if scale is None else add_kernel
    return pl.pallas_call(
        kernel,
        in_specs=([] if scale is None else [whole()]) + [whole()] * len(terms),
        out_specs=whole(),
        out_shape=jax.ShapeDtypeStruct(terms[0].shape, BF),
        compiler_params=pltpu.CompilerParams(vmem_limit_bytes=4 * MIB),
        cost_estimate=pl.CostEstimate(flops=terms[0].size * 2, bytes_accessed=terms[0].size * 4, transcendentals=0),
        name="add",
    )(*([] if scale is None else [scale]), *terms)


def shards(regions, shares, residual, basis, eigvecs, weights):
    place = Slice(regions, shares)
    core = (lax.axis_index("eig") % 2).astype(jnp.int32).reshape(1)
    blocks, vecs = basis.shape[1:3]
    count = eigvecs.shape[3]
    own = eigvecs.reshape(2, blocks * vecs, count)
    weights = weights.reshape(1, 1, count)

    part = project(residual, basis)
    chip_sum = add([part, place.swap(part)])
    sister = place.swap(own)
    holder = 0
    head = 2 * (blocks // 3)
    first = load(basis, 0, head, chip_sum)
    coarse = [chip_sum] + [place.cross(chip_sum, 1 - holder, chip=s) for s in place.chip_steps()]
    coarse, first = lax.optimization_barrier((coarse, first))

    start = holder
    active = (core == holder).astype(jnp.int32)
    value = contract(active, coarse, own, sister, weights.reshape(1, count))
    steps = list(place.region_steps())[::-1]
    for i, step in enumerate(steps):
        terms = [place.swap(value)] + [place.cross(value, holder, region=s) for s in step]
        holder = 1 - holder
        if i == 0:
            last = (start + len(steps)) % 2
            active = (core == last).astype(jnp.int32)
            turned = turn(active, [own, sister], value)
            terms, turned = lax.optimization_barrier((terms, turned))
        if i == 0 or i < len(steps) - 1:
            value = add(terms, weights if i == 0 else None)
            terms = [value]

    second = load(basis, head, blocks - head, value)
    terms, second = lax.optimization_barrier((terms, second))
    lifted = expand(active, terms, *turned, holder == start)
    terms = [place.cross(lifted, holder, chip=s) for s in place.chip_steps()]
    here = jnp.where(core == holder, lifted, total(terms).astype(BF))
    return prolong(here, place.swap(here), (first, second), residual.shape)


def solution(mesh):
    split = P(None, "region", None, "eig")
    return jax.shard_map(
        functools.partial(shards, mesh.shape["region"], mesh.shape["eig"]),
        mesh=mesh,
        in_specs=(split, split, split, P("eig")),
        out_specs=split,
        check_vma=False,
    )
```

```python
import functools
import math

import jax
import jax.numpy as jnp
from jax import lax
from jax.experimental import pallas as pl
from jax.experimental.pallas import tpu as pltpu
from jax.sharding import PartitionSpec as P

BF = jnp.bfloat16
F32 = jnp.float32
NT = (((1,), (1,)), ((), ()))
NN = (((1,), (0,)), ((), ()))
MIB = 1 << 20


def dot(left, right, dims):
    return lax.dot_general(left, right, dims, preferred_element_type=F32)


def project_kernel(res_hbm, bas_hbm, sent_ref, res_ref, bas_ref, sem):
    cols, comp = res_ref.shape[2:]
    vecs = bas_ref.shape[2]
    pair = 2 * vecs
    pairs = sem.shape[1]

    def copies(i):
        two = pl.ds(2 * i, 2)
        return (
            pltpu.make_async_copy(res_hbm.at[:, two], res_ref.at[:, two], sem.at[0, i]),
            pltpu.make_async_copy(bas_hbm.at[:, two], bas_ref.at[:, two], sem.at[1, i]),
        )

    for i in range(pairs):
        for copy in copies(i):
            copy.start()
    first = lax.broadcasted_iota(jnp.int32, (cols, pair), 1) < vecs
    for i in range(pairs):
        for copy in copies(i):
            copy.wait()
        res = res_ref[:, 2 * i : 2 * i + 2].reshape(4 * cols, comp).astype(BF)
        bas = bas_ref[:, 2 * i : 2 * i + 2].reshape(2 * pair, comp).astype(BF)
        prod = dot(res, bas, NT)

        def part(row, lane):
            lanes = slice(lane * pair, (lane + 1) * pair)
            top = prod[2 * row * cols : (2 * row + 1) * cols, lanes]
            low = prod[(2 * row + 1) * cols : (2 * row + 2) * cols, lanes]
            return jnp.where(first, top, low)

        lanes = slice(i * pair, (i + 1) * pair)
        re, im = part(0, 0) + part(1, 1), part(1, 0) - part(0, 1)
        for row, value in ((0, re), (1, im)):
            sent_ref[row, :, lanes] = value.astype(BF)


def hbm(value):
    return pltpu.with_memory_space_constraint(value, pltpu.HBM)


def whole():
    return pl.BlockSpec(memory_space=pltpu.VMEM)


def scalar():
    return pl.BlockSpec(memory_space=pltpu.SMEM)


def project(residual, basis):
    _, blocks, cols, comp = residual.shape
    vecs = basis.shape[2]
    return pl.pallas_call(
        project_kernel,
        in_specs=[pl.BlockSpec(memory_space=pltpu.HBM)] * 2,
        out_specs=whole(),
        out_shape=jax.ShapeDtypeStruct((2, cols, blocks * vecs), BF),
        scratch_shapes=[
            pltpu.VMEM(residual.shape, F32),
            pltpu.VMEM(basis.shape, F32),
            pltpu.SemaphoreType.DMA((2, blocks // 2)),
        ],
        compiler_params=pltpu.CompilerParams(vmem_limit_bytes=18 * MIB),
        cost_estimate=pl.CostEstimate(
            flops=16 * blocks * cols * vecs * comp, bytes_accessed=(residual.size + basis.size) * 4, transcendentals=0
        ),
        name="project",
    )(hbm(residual), hbm(basis))


def contract_kernel(active, own_ref, sister_ref, wgt_ref, *refs):
    *coarse_refs, out_ref = refs
    cols, depth = coarse_refs[0].shape[1:]
    count = own_ref.shape[2]

    @pl.when(active[0] == 1)
    def _():
        coarse = total([ref[...] for ref in coarse_refs]).astype(BF).reshape(2 * cols, depth)
        for i, eig_ref in enumerate((own_ref, sister_ref)):
            by_re = dot(coarse, eig_ref[0], NN)
            by_im = dot(coarse, eig_ref[1], NN)
            re = by_re[:cols] + by_im[cols:]
            im = by_re[cols:] - by_im[:cols]
            if i == 0:
                re, im = re * wgt_ref[...], im * wgt_ref[...]
            out_ref[0, :, i * count : (i + 1) * count] = re.astype(BF)
            out_ref[1, :, i * count : (i + 1) * count] = im.astype(BF)


def contract(active, coarse, own, sister, weights):
    _, cols, depth = coarse[0].shape
    count = own.shape[2]
    return pl.pallas_call(
        contract_kernel,
        in_specs=[scalar()] + [whole()] * 3 + [whole()] * len(coarse),
        out_specs=whole(),
        out_shape=jax.ShapeDtypeStruct((2, cols, 2 * count), BF),
        compiler_params=pltpu.CompilerParams(vmem_limit_bytes=4 * MIB),
        cost_estimate=pl.CostEstimate(flops=16 * cols * depth * count, bytes_accessed=own.size * 4, transcendentals=0),
        name="contract",
    )(active, own, sister, weights, *coarse)


def turn_kernel(active, *refs):
    half = len(refs) // 2
    depth, count = refs[0].shape[1:]

    @pl.when(active[0] == 1)
    def _():
        for from_ref, to_ref in zip(refs[:half], refs[half:]):
            for part in range(from_ref.shape[0]):
                for row in range(0, depth, count):
                    to_ref[part, :, row : row + count] = from_ref[part, row : row + count, :].T


def turn(active, arrays, after):
    arrays = lax.optimization_barrier((arrays, after))[0]
    shapes = [(a.shape[0], a.shape[2], a.shape[1]) for a in arrays]
    return pl.pallas_call(
        turn_kernel,
        in_specs=[scalar()] + [whole()] * len(arrays),
        out_specs=[whole()] * len(arrays),
        out_shape=[pltpu.VMEM(shape, a.dtype) for shape, a in zip(shapes, arrays)],
        compiler_params=pltpu.CompilerParams(vmem_limit_bytes=4 * MIB),
        cost_estimate=pl.CostEstimate(flops=0, bytes_accessed=sum(a.size for a in arrays) * 4, transcendentals=0),
        name="turn",
    )(active, *arrays)


def expand_kernel(own_first, active, own_ref, sister_ref, *refs):
    *wgt_refs, out_ref = refs
    cols = out_ref.shape[1]
    count = own_ref.shape[1]

    @pl.when(active[0] == 1)
    def _():
        whole_wgt = total([ref[...] for ref in wgt_refs]).astype(BF)
        re = im = None
        for i, eig_ref in enumerate((own_ref, sister_ref) if own_first else (sister_ref, own_ref)):
            weighted = whole_wgt[:, :, i * count : (i + 1) * count].reshape(2 * cols, count)
            by_re = dot(weighted, eig_ref[0], NN)
            by_im = dot(weighted, eig_ref[1], NN)
            re = by_re[:cols] - by_im[cols:] + (0 if re is None else re)
            im = by_re[cols:] + by_im[:cols] + (0 if im is None else im)
        out_ref[0] = re.astype(BF)
        out_ref[1] = im.astype(BF)


def expand(active, weighted, own, sister, own_first):
    cols = weighted[0].shape[1]
    count, depth = own.shape[1:]
    return pl.pallas_call(
        functools.partial(expand_kernel, own_first),
        in_specs=[scalar()] + [whole()] * 2 + [whole()] * len(weighted),
        out_specs=whole(),
        out_shape=jax.ShapeDtypeStruct((2, cols, depth), BF),
        compiler_params=pltpu.CompilerParams(vmem_limit_bytes=4 * MIB),
        cost_estimate=pl.CostEstimate(flops=16 * cols * depth * count, bytes_accessed=own.size * 4, transcendentals=0),
        name="expand",
    )(active, own, sister, *weighted)


def load_kernel(start, from_hbm, to_ref, sem):
    copy = pltpu.make_async_copy(from_hbm.at[:, pl.ds(start, to_ref.shape[1])], to_ref, sem)
    copy.start()
    copy.wait()


def load(value, start, size, after):
    shape = value.shape[:1] + (size,) + value.shape[2:]
    return pl.pallas_call(
        functools.partial(load_kernel, start),
        in_specs=[pl.BlockSpec(memory_space=pltpu.HBM)],
        out_specs=whole(),
        out_shape=pltpu.VMEM(shape, value.dtype),
        scratch_shapes=[pltpu.SemaphoreType.DMA],
        compiler_params=pltpu.CompilerParams(vmem_limit_bytes=4 * MIB),
        cost_estimate=pl.CostEstimate(flops=0, bytes_accessed=math.prod(shape) * 4, transcendentals=0),
        name="load",
    )(hbm(lax.optimization_barrier((value, after))[0]))


def prolong_kernel(here_ref, there_ref, *refs):
    *bas_refs, out_hbm, out_ref, sem = refs
    cols, comp = out_ref.shape[2:]
    pair = 2 * bas_refs[0].shape[2]
    pairs = sem.shape[0]
    head = bas_refs[0].shape[1] // 2
    first = lax.broadcasted_iota(jnp.int32, (cols, pair), 1) < pair // 2

    def copy(i):
        two = pl.ds(2 * i, 2)
        return pltpu.make_async_copy(out_ref.at[:, two], out_hbm.at[:, two], sem.at[i])

    for i in range(pairs):
        lanes = slice(i * pair, (i + 1) * pair)
        re, im = (total([ref[row, :, lanes] for ref in (here_ref, there_ref)]).astype(BF) for row in range(2))
        none = jnp.zeros_like(re)
        re0, re1 = jnp.where(first, re, none), jnp.where(first, none, re)
        im0, im1 = jnp.where(first, im, none), jnp.where(first, none, im)
        left = jnp.concatenate(
            [
                jnp.concatenate([re0, re1, im0, im1], axis=0),
                jnp.concatenate([-im0, -im1, re0, re1], axis=0),
            ],
            axis=1,
        )
        part, j = (0, i) if i < head else (1, i - head)
        bas = bas_refs[part][:, 2 * j : 2 * j + 2].reshape(2 * pair, comp).astype(BF)
        out_ref[:, 2 * i : 2 * i + 2] = dot(left, bas, NN).reshape(2, 2, cols, comp)
        copy(i).start()
    for i in range(pairs):
        copy(i).wait()


def prolong(here, there, basis, shape):
    vecs, comp = basis[0].shape[2:]
    cols = here.shape[1]
    pairs = shape[1] // 2
    return pl.pallas_call(
        prolong_kernel,
        in_specs=[whole()] * (2 + len(basis)),
        out_specs=pl.BlockSpec(memory_space=pltpu.HBM),
        out_shape=jax.ShapeDtypeStruct(shape, F32),
        scratch_shapes=[pltpu.VMEM(shape, F32), pltpu.SemaphoreType.DMA((pairs,))],
        compiler_params=pltpu.CompilerParams(vmem_limit_bytes=8 * MIB),
        cost_estimate=pl.CostEstimate(flops=64 * pairs * cols * vecs * comp, bytes_accessed=pairs * cols * comp * 16, transcendentals=0),
        name="prolong",
    )(here, there, *basis)


class Slice:
    def __init__(self, regions, shares):
        self.regions, self.shares = regions, shares

    def swap(self, value):
        return lax.ppermute(value, "eig", [(i, i ^ 1) for i in range(self.shares)])

    def cross(self, value, sender, region=0, chip=0):
        pairs = []
        for i in range(self.regions * self.shares):
            far = (i ^ (region * self.shares) ^ (2 * chip)) ^ 1
            pairs.append((i, far if i % 2 == sender else i ^ 1))
        return lax.ppermute(value, ("region", "eig"), pairs)

    def region_steps(self):
        step = 1
        while step < self.regions:
            four = 2 * step < self.regions
            yield [2 * step, step, 3 * step] if four else [step]
            step *= 4 if four else 2

    def chip_steps(self):
        return range(1, self.shares // 2)


def total(terms):
    value = terms[0].astype(F32)
    for term in terms[1:]:
        value = value + term.astype(F32)
    return value


def add_kernel(scale_ref, *refs):
    *term_refs, out_ref = refs
    value = total([ref[...] for ref in term_refs])
    half = out_ref.shape[2] // 2
    if scale_ref is None:
        out_ref[...] = value.astype(BF)
    else:
        out_ref[:, :, :half] = value[:, :, :half].astype(BF)
        out_ref[:, :, half:] = (value[:, :, half:] * scale_ref[...]).astype(BF)


def add(terms, scale=None):
    kernel = functools.partial(add_kernel, None) if scale is None else add_kernel
    return pl.pallas_call(
        kernel,
        in_specs=([] if scale is None else [whole()]) + [whole()] * len(terms),
        out_specs=whole(),
        out_shape=jax.ShapeDtypeStruct(terms[0].shape, BF),
        compiler_params=pltpu.CompilerParams(vmem_limit_bytes=4 * MIB),
        cost_estimate=pl.CostEstimate(flops=terms[0].size * 2, bytes_accessed=terms[0].size * 4, transcendentals=0),
        name="add",
    )(*([] if scale is None else [scale]), *terms)


def shards(regions, shares, residual, basis, eigvecs, weights):
    place = Slice(regions, shares)
    core = (lax.axis_index("eig") % 2).astype(jnp.int32).reshape(1)
    blocks, vecs = basis.shape[1:3]
    count = eigvecs.shape[3]
    own = eigvecs.reshape(2, blocks * vecs, count)
    weights = weights.reshape(1, 1, count)

    part = project(residual, basis)
    chip_sum = add([part, place.swap(part)])
    sister = place.swap(own)
    holder = 0
    head = 2 * (blocks * 5 // 24)
    first = load(basis, 0, head, chip_sum)
    coarse = [chip_sum] + [place.cross(chip_sum, 1 - holder, chip=s) for s in place.chip_steps()]
    coarse, first = lax.optimization_barrier((coarse, first))

    start = holder
    active = (core == holder).astype(jnp.int32)
    value = contract(active, coarse, own, sister, weights.reshape(1, count))
    steps = list(place.region_steps())[::-1]
    for i, step in enumerate(steps):
        terms = [place.swap(value)] + [place.cross(value, holder, region=s) for s in step]
        holder = 1 - holder
        if i == 0:
            last = (start + len(steps)) % 2
            active = (core == last).astype(jnp.int32)
            turned = turn(active, [own, sister], value)
            terms, turned = lax.optimization_barrier((terms, turned))
        if i == 0 or i < len(steps) - 1:
            value = add(terms, weights if i == 0 else None)
            terms = [value]

    second = load(basis, head, blocks - head, value)
    terms, second = lax.optimization_barrier((terms, second))
    lifted = expand(active, terms, *turned, holder == start)
    terms = [place.cross(lifted, holder, chip=s) for s in place.chip_steps()]
    here = jnp.where(core == holder, lifted, total(terms).astype(BF))
    return prolong(here, place.swap(here), (first, second), residual.shape)


def solution(mesh):
    split = P(None, "region", None, "eig")
    return jax.shard_map(
        functools.partial(shards, mesh.shape["region"], mesh.shape["eig"]),
        mesh=mesh,
        in_specs=(split, split, split, P("eig")),
        out_specs=split,
        check_vma=False,
    )
```

```python
import functools
import math

import jax
import jax.numpy as jnp
from jax import lax
from jax.experimental import pallas as pl
from jax.experimental.pallas import tpu as pltpu
from jax.sharding import PartitionSpec as P

BF = jnp.bfloat16
F32 = jnp.float32
NT = (((1,), (1,)), ((), ()))
NN = (((1,), (0,)), ((), ()))
MIB = 1 << 20


def dot(left, right, dims):
    return lax.dot_general(left, right, dims, preferred_element_type=F32)


def project_kernel(res_hbm, bas_hbm, sent_ref, res_ref, bas_ref, sem):
    cols, comp = res_ref.shape[2:]
    vecs = bas_ref.shape[2]
    pair = 2 * vecs
    pairs = sem.shape[1]

    def copies(i):
        two = pl.ds(2 * i, 2)
        return (
            pltpu.make_async_copy(res_hbm.at[:, two], res_ref.at[:, two], sem.at[0, i]),
            pltpu.make_async_copy(bas_hbm.at[:, two], bas_ref.at[:, two], sem.at[1, i]),
        )

    for i in range(pairs):
        for copy in copies(i):
            copy.start()
    first = lax.broadcasted_iota(jnp.int32, (cols, pair), 1) < vecs
    for i in range(pairs):
        for copy in copies(i):
            copy.wait()
        res = res_ref[:, 2 * i : 2 * i + 2].reshape(4 * cols, comp).astype(BF)
        bas = bas_ref[:, 2 * i : 2 * i + 2].reshape(2 * pair, comp).astype(BF)
        prod = dot(res, bas, NT)

        def part(row, lane):
            lanes = slice(lane * pair, (lane + 1) * pair)
            top = prod[2 * row * cols : (2 * row + 1) * cols, lanes]
            low = prod[(2 * row + 1) * cols : (2 * row + 2) * cols, lanes]
            return jnp.where(first, top, low)

        lanes = slice(i * pair, (i + 1) * pair)
        re, im = part(0, 0) + part(1, 1), part(1, 0) - part(0, 1)
        for row, value in ((0, re), (1, im)):
            sent_ref[row, :, lanes] = value.astype(BF)


def hbm(value):
    return pltpu.with_memory_space_constraint(value, pltpu.HBM)


def whole():
    return pl.BlockSpec(memory_space=pltpu.VMEM)


def scalar():
    return pl.BlockSpec(memory_space=pltpu.SMEM)


def project(residual, basis):
    _, blocks, cols, comp = residual.shape
    vecs = basis.shape[2]
    return pl.pallas_call(
        project_kernel,
        in_specs=[pl.BlockSpec(memory_space=pltpu.HBM)] * 2,
        out_specs=whole(),
        out_shape=jax.ShapeDtypeStruct((2, cols, blocks * vecs), BF),
        scratch_shapes=[
            pltpu.VMEM(residual.shape, F32),
            pltpu.VMEM(basis.shape, F32),
            pltpu.SemaphoreType.DMA((2, blocks // 2)),
        ],
        compiler_params=pltpu.CompilerParams(vmem_limit_bytes=18 * MIB),
        cost_estimate=pl.CostEstimate(
            flops=16 * blocks * cols * vecs * comp, bytes_accessed=(residual.size + basis.size) * 4, transcendentals=0
        ),
        name="project",
    )(hbm(residual), hbm(basis))


def contract_kernel(active, own_ref, sister_ref, wgt_ref, *refs):
    *coarse_refs, out_ref = refs
    cols, depth = coarse_refs[0].shape[1:]
    count = own_ref.shape[2]

    @pl.when(active[0] == 1)
    def _():
        coarse = total([ref[...] for ref in coarse_refs]).astype(BF).reshape(2 * cols, depth)
        for i, eig_ref in enumerate((own_ref, sister_ref)):
            by_re = dot(coarse, eig_ref[0], NN)
            by_im = dot(coarse, eig_ref[1], NN)
            re = by_re[:cols] + by_im[cols:]
            im = by_re[cols:] - by_im[:cols]
            if i == 0:
                re, im = re * wgt_ref[...], im * wgt_ref[...]
            out_ref[0, :, i * count : (i + 1) * count] = re.astype(BF)
            out_ref[1, :, i * count : (i + 1) * count] = im.astype(BF)


def contract(active, coarse, own, sister, weights):
    _, cols, depth = coarse[0].shape
    count = own.shape[2]
    return pl.pallas_call(
        contract_kernel,
        in_specs=[scalar()] + [whole()] * 3 + [whole()] * len(coarse),
        out_specs=whole(),
        out_shape=jax.ShapeDtypeStruct((2, cols, 2 * count), BF),
        compiler_params=pltpu.CompilerParams(vmem_limit_bytes=4 * MIB),
        cost_estimate=pl.CostEstimate(flops=16 * cols * depth * count, bytes_accessed=own.size * 4, transcendentals=0),
        name="contract",
    )(active, own, sister, weights, *coarse)


def turn_kernel(active, *refs):
    half = len(refs) // 2
    depth, count = refs[0].shape[1:]

    @pl.when(active[0] == 1)
    def _():
        for from_ref, to_ref in zip(refs[:half], refs[half:]):
            for part in range(from_ref.shape[0]):
                for row in range(0, depth, count):
                    to_ref[part, :, row : row + count] = from_ref[part, row : row + count, :].T


def turn(active, arrays, after):
    arrays = lax.optimization_barrier((arrays, after))[0]
    shapes = [(a.shape[0], a.shape[2], a.shape[1]) for a in arrays]
    return pl.pallas_call(
        turn_kernel,
        in_specs=[scalar()] + [whole()] * len(arrays),
        out_specs=[whole()] * len(arrays),
        out_shape=[pltpu.VMEM(shape, a.dtype) for shape, a in zip(shapes, arrays)],
        compiler_params=pltpu.CompilerParams(vmem_limit_bytes=4 * MIB),
        cost_estimate=pl.CostEstimate(flops=0, bytes_accessed=sum(a.size for a in arrays) * 4, transcendentals=0),
        name="turn",
    )(active, *arrays)


def expand_kernel(own_first, active, own_ref, sister_ref, *refs):
    *wgt_refs, out_ref = refs
    cols = out_ref.shape[1]
    count = own_ref.shape[1]

    @pl.when(active[0] == 1)
    def _():
        whole_wgt = total([ref[...] for ref in wgt_refs]).astype(BF)
        re = im = None
        for i, eig_ref in enumerate((own_ref, sister_ref) if own_first else (sister_ref, own_ref)):
            weighted = whole_wgt[:, :, i * count : (i + 1) * count].reshape(2 * cols, count)
            by_re = dot(weighted, eig_ref[0], NN)
            by_im = dot(weighted, eig_ref[1], NN)
            re = by_re[:cols] - by_im[cols:] + (0 if re is None else re)
            im = by_re[cols:] + by_im[:cols] + (0 if im is None else im)
        out_ref[0] = re.astype(BF)
        out_ref[1] = im.astype(BF)


def expand(active, weighted, own, sister, own_first):
    cols = weighted[0].shape[1]
    count, depth = own.shape[1:]
    return pl.pallas_call(
        functools.partial(expand_kernel, own_first),
        in_specs=[scalar()] + [whole()] * 2 + [whole()] * len(weighted),
        out_specs=whole(),
        out_shape=jax.ShapeDtypeStruct((2, cols, depth), BF),
        compiler_params=pltpu.CompilerParams(vmem_limit_bytes=4 * MIB),
        cost_estimate=pl.CostEstimate(flops=16 * cols * depth * count, bytes_accessed=own.size * 4, transcendentals=0),
        name="expand",
    )(active, own, sister, *weighted)


def load_kernel(start, from_hbm, to_ref, sem):
    copy = pltpu.make_async_copy(from_hbm.at[:, pl.ds(start, to_ref.shape[1])], to_ref, sem)
    copy.start()
    copy.wait()


def load(value, start, size, after):
    shape = value.shape[:1] + (size,) + value.shape[2:]
    return pl.pallas_call(
        functools.partial(load_kernel, start),
        in_specs=[pl.BlockSpec(memory_space=pltpu.HBM)],
        out_specs=whole(),
        out_shape=pltpu.VMEM(shape, value.dtype),
        scratch_shapes=[pltpu.SemaphoreType.DMA],
        compiler_params=pltpu.CompilerParams(vmem_limit_bytes=4 * MIB),
        cost_estimate=pl.CostEstimate(flops=0, bytes_accessed=math.prod(shape) * 4, transcendentals=0),
        name="load",
    )(hbm(lax.optimization_barrier((value, after))[0]))


def prolong_kernel(here_ref, there_ref, *refs):
    *bas_refs, out_hbm, out_ref, sem = refs
    cols, comp = out_ref.shape[2:]
    pair = 2 * bas_refs[0].shape[2]
    pairs = sem.shape[0]
    head = bas_refs[0].shape[1] // 2
    first = lax.broadcasted_iota(jnp.int32, (cols, pair), 1) < pair // 2

    def copy(i):
        two = pl.ds(2 * i, 2)
        return pltpu.make_async_copy(out_ref.at[:, two], out_hbm.at[:, two], sem.at[i])

    for i in range(pairs):
        lanes = slice(i * pair, (i + 1) * pair)
        re, im = (total([ref[row, :, lanes] for ref in (here_ref, there_ref)]).astype(BF) for row in range(2))
        none = jnp.zeros_like(re)
        re0, re1 = jnp.where(first, re, none), jnp.where(first, none, re)
        im0, im1 = jnp.where(first, im, none), jnp.where(first, none, im)
        left = jnp.concatenate(
            [
                jnp.concatenate([re0, re1, im0, im1], axis=0),
                jnp.concatenate([-im0, -im1, re0, re1], axis=0),
            ],
            axis=1,
        )
        part, j = (0, i) if i < head else (1, i - head)
        bas = bas_refs[part][:, 2 * j : 2 * j + 2].reshape(2 * pair, comp).astype(BF)
        out_ref[:, 2 * i : 2 * i + 2] = dot(left, bas, NN).reshape(2, 2, cols, comp)
        copy(i).start()
    for i in range(pairs):
        copy(i).wait()


def prolong(here, there, basis, shape):
    vecs, comp = basis[0].shape[2:]
    cols = here.shape[1]
    pairs = shape[1] // 2
    return pl.pallas_call(
        prolong_kernel,
        in_specs=[whole()] * (2 + len(basis)),
        out_specs=pl.BlockSpec(memory_space=pltpu.HBM),
        out_shape=jax.ShapeDtypeStruct(shape, F32),
        scratch_shapes=[pltpu.VMEM(shape, F32), pltpu.SemaphoreType.DMA((pairs,))],
        compiler_params=pltpu.CompilerParams(vmem_limit_bytes=8 * MIB),
        cost_estimate=pl.CostEstimate(flops=64 * pairs * cols * vecs * comp, bytes_accessed=pairs * cols * comp * 16, transcendentals=0),
        name="prolong",
    )(here, there, *basis)


class Slice:
    def __init__(self, regions, shares):
        self.regions, self.shares = regions, shares

    def swap(self, value):
        return lax.ppermute(value, "eig", [(i, i ^ 1) for i in range(self.shares)])

    def cross(self, value, sender, region=0, chip=0):
        pairs = []
        for i in range(self.regions * self.shares):
            far = (i ^ (region * self.shares) ^ (2 * chip)) ^ 1
            pairs.append((i, far if i % 2 == sender else i ^ 1))
        return lax.ppermute(value, ("region", "eig"), pairs)

    def region_steps(self):
        step = 1
        while step < self.regions:
            four = 2 * step < self.regions
            yield [2 * step, step, 3 * step] if four else [step]
            step *= 4 if four else 2

    def chip_steps(self):
        return range(1, self.shares // 2)


def total(terms):
    value = terms[0].astype(F32)
    for term in terms[1:]:
        value = value + term.astype(F32)
    return value


def add_kernel(scale_ref, *refs):
    *term_refs, out_ref = refs
    value = total([ref[...] for ref in term_refs])
    half = out_ref.shape[2] // 2
    if scale_ref is None:
        out_ref[...] = value.astype(BF)
    else:
        out_ref[:, :, :half] = value[:, :, :half].astype(BF)
        out_ref[:, :, half:] = (value[:, :, half:] * scale_ref[...]).astype(BF)


def add(terms, scale=None):
    kernel = functools.partial(add_kernel, None) if scale is None else add_kernel
    return pl.pallas_call(
        kernel,
        in_specs=([] if scale is None else [whole()]) + [whole()] * len(terms),
        out_specs=whole(),
        out_shape=jax.ShapeDtypeStruct(terms[0].shape, BF),
        compiler_params=pltpu.CompilerParams(vmem_limit_bytes=4 * MIB),
        cost_estimate=pl.CostEstimate(flops=terms[0].size * 2, bytes_accessed=terms[0].size * 4, transcendentals=0),
        name="add",
    )(*([] if scale is None else [scale]), *terms)


def shards(regions, shares, residual, basis, eigvecs, weights):
    place = Slice(regions, shares)
    core = (lax.axis_index("eig") % 2).astype(jnp.int32).reshape(1)
    blocks, vecs = basis.shape[1:3]
    count = eigvecs.shape[3]
    own = eigvecs.reshape(2, blocks * vecs, count)
    weights = weights.reshape(1, 1, count)

    part = project(residual, basis)
    chip_sum = add([part, place.swap(part)])
    sister = place.swap(own)
    holder = 0
    head = 2 * (blocks // 3)
    first = load(basis, 0, head, chip_sum)
    coarse = [chip_sum] + [place.cross(chip_sum, 1 - holder, chip=s) for s in place.chip_steps()]
    steps = list(place.region_steps())[::-1]
    last = (core == (holder + len(steps)) % 2).astype(jnp.int32)
    turned = turn(last, [own, sister], first)
    coarse, first, turned = lax.optimization_barrier((coarse, first, turned))

    start = holder
    active = (core == holder).astype(jnp.int32)
    value = contract(active, coarse, own, sister, weights.reshape(1, count))
    for i, step in enumerate(steps):
        terms = [place.swap(value)] + [place.cross(value, holder, region=s) for s in step]
        holder = 1 - holder
        if i == 0 or i < len(steps) - 1:
            value = add(terms, weights if i == 0 else None)
            terms = [value]

    second = load(basis, head, blocks - head, value)
    terms, second = lax.optimization_barrier((terms, second))
    lifted = expand(last, terms, *turned, holder == start)
    terms = [place.cross(lifted, holder, chip=s) for s in place.chip_steps()]
    here = jnp.where(core == holder, lifted, total(terms).astype(BF))
    return prolong(here, place.swap(here), (first, second), residual.shape)


def solution(mesh):
    split = P(None, "region", None, "eig")
    return jax.shard_map(
        functools.partial(shards, mesh.shape["region"], mesh.shape["eig"]),
        mesh=mesh,
        in_specs=(split, split, split, P("eig")),
        out_specs=split,
        check_vma=False,
    )
```
